32 devices in a mesh: ctx: 16 (over z, y, x), head: 2 (over core).
Axes of the slice: x: 2, y: 2, z: 4, core: 2. Of those that a mesh axis runs over, the one named last changes fastest.
Arguments:
- placement: int32 [16], replicated, may hold values from 0 to 15, each once
- placed_queries: bfloat16 [4096, 4096], P('ctx', 'head'), may hold values from -160 to 160
- placed_keys: bfloat16 [4096, 1024], P('ctx', 'head'), may hold values from -4.5 to 4.5
- placed_values: bfloat16 [4096, 1024], P('ctx', 'head'), may hold values from -6 to 6
- out_weight: bfloat16 [4096, 4096], P('head', 'ctx'), may hold values from -0.125 to 0.125
Outputs:
- attention_out: bfloat16 [4096, 4096], P('ctx', 'head')
The draws below stay inside these ranges and needn't reach their ends.
Inputs may be any that keep to these rules, and one draw needn't show every extreme that they name: placement holds each of 0 .. 15 once.
All inputs are finite; a program needn't handle non-finite values.
Results may differ from the reference program's by a relative error of at most 0.015.
Values may be sent and summed in bfloat16 or wider, within the bound.
A program may use at most 64 MiB of HBM per device.

```python
import jax
import jax.numpy as jnp
from jax import lax

D = 4096
QUERY_HEADS = 32
KEY_VALUE_HEADS = 8
HEAD_FEATURES = 128
TOKENS_PER_PART = 256
SEQUENCE_TOKENS = 4096
N_CTX = 16
N_HEAD = 2


def shared_keys(key):
    random_seed_key = jax.random.fold_in(key, 11)
    sampled = jnp.clip(jax.random.normal(random_seed_key, (SEQUENCE_TOKENS, KEY_VALUE_HEADS * HEAD_FEATURES), jnp.float32), -4.5, 4.5)
    return sampled


def draw_placed_keys(key, part):
    return shared_keys(key).astype(jnp.bfloat16)


def draw_placed_queries(key, part):
    sampled = jnp.clip(jax.random.normal(jax.random.fold_in(key, 13), (SEQUENCE_TOKENS, QUERY_HEADS * HEAD_FEATURES), jnp.float32), -4.5, 4.5)
    return sampled.astype(jnp.bfloat16)


def with_spikes(values, stream_key, source, target, parts, factor):
    def block_of(dim):
        return (jnp.arange(values.shape[dim]) // (values.shape[dim] // parts)).reshape((-1,) + (1,) * (values.ndim - 1 - dim))

    near = jax.random.permutation(stream_key, parts)[block_of(target)]
    other_side = (block_of(target) + parts // 2) % parts
    return jnp.where((block_of(source) == near) | (block_of(source) == other_side), factor * values, values)


def block_levels(rng, shape, cuts, low, top_value):
    factor_of, own = 1.0, jax.random.fold_in(rng, 6)
    for axis_at, shards_of in cuts:
        steps = jnp.exp(jax.random.uniform(jax.random.fold_in(own, axis_at), (shards_of,), jnp.float32, low / len(cuts), top_value / len(cuts)))
        factor_of = factor_of * jnp.repeat(steps, shape[axis_at] // shards_of).reshape([-1 if axis == axis_at else 1 for axis in range(len(shape))])
    return factor_of


def centred(rng, shape, scale, reach, cuts=(), held_as=jnp.bfloat16):
    values = scale * jax.random.normal(rng, shape, jnp.float32)
    if cuts:
        values = values * block_levels(rng, shape, cuts, -0.22, 0.18)
    return jnp.clip(values, -reach, reach).astype(held_as)


def gaussian_with(key, shape, deviation, limit, cuts, heavy, kind=jnp.bfloat16):
    drawn = deviation * jax.random.normal(key, shape, jnp.float32)
    if cuts:
        drawn = drawn * block_levels(key, shape, cuts, -0.22, 0.18)
    return jnp.clip(with_spikes(drawn, jax.random.fold_in(key, 3), *heavy), -limit, limit).astype(kind)


def setup_inputs(seed: int = 0) -> dict:
    keys = jax.random.split(jax.random.key(seed), 6)
    placement = jax.random.permutation(keys[0], N_CTX).astype(jnp.int32)
    placed_queries = draw_placed_queries(jax.random.fold_in(keys[5], 71), 0)
    placed_keys = draw_placed_keys(jax.random.fold_in(keys[5], 71), 0)
    placed_values = centred(keys[3], (SEQUENCE_TOKENS, KEY_VALUE_HEADS * HEAD_FEATURES), 1.0, 6.0, ((0, 16), (1, 2)))
    out_weight = gaussian_with(keys[4], (QUERY_HEADS * HEAD_FEATURES, D), (QUERY_HEADS * HEAD_FEATURES) ** -0.5, 0.125, ((0, 2), (1, 16)), (0, 1, 16, 2.0))
    return {"placement": placement, "placed_queries": placed_queries, "placed_keys": placed_keys, "placed_values": placed_values, "out_weight": out_weight}


masked_score = -1.0e30


def causal_softmax(placement, placed_queries, placed_keys, placed_values):
    order_indices = jnp.argsort(placement)
    model_width = QUERY_HEADS * HEAD_FEATURES
    common_across = QUERY_HEADS // KEY_VALUE_HEADS
    sequence_queries = placed_queries.reshape(N_CTX, TOKENS_PER_PART, model_width)[order_indices].reshape(SEQUENCE_TOKENS, KEY_VALUE_HEADS, common_across, HEAD_FEATURES)
    sequence_keys = placed_keys.reshape(N_CTX, TOKENS_PER_PART, KEY_VALUE_HEADS * HEAD_FEATURES)[order_indices].reshape(SEQUENCE_TOKENS, KEY_VALUE_HEADS, HEAD_FEATURES)
    sequence_values = placed_values.reshape(N_CTX, TOKENS_PER_PART, KEY_VALUE_HEADS * HEAD_FEATURES)[order_indices].reshape(SEQUENCE_TOKENS, KEY_VALUE_HEADS, HEAD_FEATURES)
    block_rows = SEQUENCE_TOKENS // 16
    results = []
    for member in range(16):
        low_row = member * block_rows
        high_row = low_row + block_rows
        query_block = jnp.transpose(sequence_queries[low_row:high_row], (1, 2, 0, 3)).astype(jnp.float32)
        key_block = jnp.transpose(sequence_keys[:high_row], (1, 0, 2)).astype(jnp.float32)
        value_block = jnp.transpose(sequence_values[:high_row], (1, 0, 2)).astype(jnp.float32)
        query_pos = low_row + jnp.arange(block_rows, dtype=jnp.int32)
        key_pos = jnp.arange(high_row, dtype=jnp.int32)
        allowed = key_pos[None, :] <= query_pos[:, None]

        def one_head(operands):
            head_queries, head_keys, head_values = operands
            scores = jnp.einsum("grd,sd->grs", head_queries, head_keys) * (HEAD_FEATURES ** -0.5)
            scores = jnp.where(allowed, scores, masked_score)
            peak = jnp.max(scores, axis=-1, keepdims=True)
            weights = jnp.where(allowed, jnp.exp(scores - peak), 0.0)
            norm_sum = jnp.sum(weights, axis=-1)
            rounded = lax.optimization_barrier(weights.astype(jnp.bfloat16)).astype(jnp.float32)
            return jnp.einsum("grs,sd->grd", rounded, head_values) / norm_sum[..., None]

        block_out = lax.map(one_head, (query_block, key_block, value_block))
        results.append(jnp.transpose(block_out, (2, 0, 1, 3)).reshape(block_rows, model_width).astype(jnp.bfloat16))
    seq_out = jnp.concatenate(results, axis=0)
    return seq_out.reshape(N_CTX, TOKENS_PER_PART, model_width)[placement].reshape(SEQUENCE_TOKENS, model_width)


def reference(placement, placed_queries, placed_keys, placed_values, out_weight):
    hidden = causal_softmax(placement, placed_queries, placed_keys, placed_values)
    width_dev = QUERY_HEADS * HEAD_FEATURES // N_HEAD
    summed = jnp.zeros((SEQUENCE_TOKENS, D), jnp.float32)
    for member in range(N_HEAD):
        term = jnp.dot(hidden[:, member * width_dev:(member + 1) * width_dev], out_weight[member * width_dev:(member + 1) * width_dev], preferred_element_type=jnp.float32)
        summed = summed + lax.optimization_barrier(term.astype(jnp.bfloat16)).astype(jnp.float32)
    return summed.astype(jnp.bfloat16)
```

```python
import functools

import jax
import jax.numpy as jnp
from jax import lax
from jax.experimental import pallas as pl
from jax.experimental.pallas import tpu as pltpu
from jax.sharding import PartitionSpec as P

HEAD_FEATURES = 128
PLANE = 4
LOG2_E = 1.4426950408889634
MESH = pl.DeviceIdType.MESH
lowest = -1e30
vmem_limit = 60 * 1024 * 1024


def attend_kernel(scale, place_ref, own_ref, q_ref, k_ref, v_ref, o_ref, stacked, peak, total, acc):
    blocks, rows, _ = k_ref.shape
    heads = q_ref.shape[1] // HEAD_FEATURES
    for i in range(heads):
        stacked[i * rows:(i + 1) * rows, :] = q_ref[:, i * HEAD_FEATURES:(i + 1) * HEAD_FEATURES]
    peak[...] = jnp.full_like(peak, lowest)
    total[...] = jnp.zeros_like(total)
    acc[...] = jnp.zeros_like(acc)
    mine = own_ref[0]

    def update(j, diagonal):
        keys = k_ref[j]
        values = v_ref[j]
        for i in range(heads):
            cols = slice(i * rows, (i + 1) * rows)
            scores = lax.dot_general(
                keys, stacked[cols, :], (((1,), (1,)), ((), ())), preferred_element_type=jnp.float32
            )
            if diagonal:
                key_at = lax.broadcasted_iota(jnp.int32, scores.shape, 0)
                query_at = lax.broadcasted_iota(jnp.int32, scores.shape, 1)
                scores = jnp.where(key_at <= query_at, scores, lowest)
            old = peak[:, cols]
            new = jnp.maximum(old, jnp.max(scores, axis=0, keepdims=True))
            weights = jnp.exp2((scores - new) * scale)
            shrink = jnp.exp2((old - new) * scale)
            peak[:, cols] = new
            total[:, cols] = total[:, cols] * shrink + jnp.sum(weights, axis=0, keepdims=True)
            acc[:, cols] = acc[:, cols] * shrink + lax.dot_general(
                values, weights.astype(jnp.bfloat16), (((0,), (0,)), ((), ())),
                preferred_element_type=jnp.float32,
            )

    def step(j, carry):
        at = place_ref[j]

        @pl.when(at < mine)
        def _():
            update(j, False)

        @pl.when(at == mine)
        def _():
            update(j, True)

        return carry

    lax.fori_loop(0, blocks, step, 0)
    for i in range(heads):
        cols = slice(i * rows, (i + 1) * rows)
        out = acc[:, cols] / total[:, cols]
        o_ref[:, i * HEAD_FEATURES:(i + 1) * HEAD_FEATURES] = out.T.astype(o_ref.dtype)


def attend(placement, own_block, queries, keys, values):
    blocks, rows, width = keys.shape
    kv_heads = width // HEAD_FEATURES
    group = queries.shape[1] // kv_heads
    common = group // HEAD_FEATURES
    scale = HEAD_FEATURES ** (-0.5) * LOG2_E
    return pl.pallas_call(
        functools.partial(attend_kernel, scale),
        out_shape=jax.ShapeDtypeStruct(queries.shape, queries.dtype),
        grid_spec=pltpu.PrefetchScalarGridSpec(
            num_scalar_prefetch=2,
            grid=(kv_heads,),
            in_specs=[
                pl.BlockSpec((rows, group), lambda g, *_: (0, g)),
                pl.BlockSpec((blocks, rows, HEAD_FEATURES), lambda g, *_: (0, 0, g)),
                pl.BlockSpec((blocks, rows, HEAD_FEATURES), lambda g, *_: (0, 0, g)),
            ],
            out_specs=pl.BlockSpec((rows, group), lambda g, *_: (0, g)),
            scratch_shapes=[
                pltpu.VMEM((common * rows, HEAD_FEATURES), jnp.bfloat16),
                pltpu.VMEM((1, common * rows), jnp.float32),
                pltpu.VMEM((1, common * rows), jnp.float32),
                pltpu.VMEM((HEAD_FEATURES, common * rows), jnp.float32),
            ],
        ),
        compiler_params=pltpu.CompilerParams(vmem_limit_bytes=vmem_limit),
        cost_estimate=pl.CostEstimate(
            flops=4 * blocks * rows * rows * queries.shape[1],
            bytes_accessed=4 * (keys.size + queries.size),
            transcendentals=blocks * rows * rows * kv_heads * common,
        ),
    )(placement, own_block, queries, keys, values)


def place_of(depth):
    me = lax.axis_index("ctx")
    z = me // PLANE
    p = me % PLANE
    flip_x = p + 1 - 2 * (p % 2)
    flip_y = (p + 2) % PLANE
    return z, p, flip_x, flip_y, (flip_x + 2) % PLANE


class Copies:
    def __init__(self):
        self.started = []

    def start(self, condition, make):
        @pl.when(condition)
        def _():
            make().start()

        self.started.append((condition, make))

    def finish(self):
        for condition, make in self.started:
            @pl.when(condition)
            def _(make=make):
                make().wait_send()


def remote(src, dst, send, recv, target):
    return pltpu.make_async_remote_copy(
        src_ref=src, dst_ref=dst, send_sem=send, recv_sem=recv,
        device_id={"ctx": target}, device_id_type=MESH,
    )


def gather_kernel(depth, half, k_ref, v_ref, w_ref, k_all, v_all, w_all,
                  own_sem, line_send, plane_send, relay_send, recv, w_send, w_recv):
    z, p, px, py, pd = place_of(depth)
    me = z * PLANE + p
    barrier = pltpu.get_barrier_semaphore()
    greeted = (
        z * PLANE + px, z * PLANE + py,
        (z + 1) % depth * PLANE + p, (z + depth - 1) % depth * PLANE + p,
    )
    for other in greeted:
        pl.semaphore_signal(barrier, inc=1, device_id={"ctx": other}, device_id_type=MESH)
    pl.semaphore_wait(barrier, len(greeted))

    w_own = w_ref.at[pl.ds(0, half), :]
    locals_ = [
        pltpu.make_async_copy(k_ref, k_all.at[me], own_sem.at[0]),
        pltpu.make_async_copy(v_ref, v_all.at[me], own_sem.at[1]),
        pltpu.make_async_copy(w_own, w_all.at[z], own_sem.at[2]),
    ]
    copies = Copies()
    pairs = ((k_ref, k_all), (v_ref, v_all))

    def arrived(array, source):
        ref = pairs[array][1].at[source]
        remote(ref, ref, own_sem.at[0], recv.at[array, source], me).wait_recv()

    def move(array, source, own, send, target):
        dst = pairs[array][1].at[source]
        src = pairs[array][0] if own else dst
        return remote(src, dst, send, recv.at[array, source], target)

    def line(array, zs, own, up):
        target = (z + 1 if up else z - 1) * PLANE + p
        return move(array, zs * PLANE + p, own, line_send.at[array, zs, int(up)], target)

    def plane(array, zs, own, axis):
        target = z * PLANE + (px if axis == 0 else py)
        return move(array, zs * PLANE + p, own, plane_send.at[array, zs, axis], target)

    def relay(array, zs):
        source, target = (px, py) if array == 0 else (py, px)
        return move(array, zs * PLANE + source, False, relay_send.at[array, zs], z * PLANE + target)

    def weight(zs, own, up):
        target = (z + 1 if up else z - 1) * PLANE + p
        dst = w_all.at[zs]
        return remote(w_own if own else dst, dst, w_send.at[zs, int(up)], w_recv.at[zs], target)

    above = z + 1 < depth
    below = z > 0
    always = z >= 0
    for array in range(2):
        copies.start(above, functools.partial(line, array, z, True, True))
        copies.start(below, functools.partial(line, array, z, True, False))
    for array in range(2):
        for axis in range(2):
            copies.start(always, functools.partial(plane, array, z, True, axis))
    for copy in locals_:
        copy.start()

    def pass_on(t):
        for up in (True, False):
            zs = z - t if up else z + t
            there = z >= t if up else zs < depth

            @pl.when(there)
            def _(zs=zs):
                for array in range(2):
                    arrived(array, zs * PLANE + p)

            on = there & (above if up else below)
            for array in range(2):
                copies.start(on, functools.partial(line, array, zs, False, up))
            for array in range(2):
                for axis in range(2):
                    copies.start(there, functools.partial(plane, array, zs, False, axis))

    def pass_across(t):
        for up in (True, False)[: 1 if t == 0 else 2]:
            zs = z - t if up else z + t
            there = z >= t if up else zs < depth

            @pl.when(there)
            def _(zs=zs):
                arrived(0, zs * PLANE + px)
                arrived(1, zs * PLANE + py)

            for array in range(2):
                copies.start(there, functools.partial(relay, array, zs))

    def pass_weight(t):
        if t == 0:
            copies.start(above, functools.partial(weight, z, True, True))
            copies.start(below, functools.partial(weight, z, True, False))
            return
        for up in (True, False):
            zs = z - t if up else z + t
            there = z >= t if up else zs < depth

            @pl.when(there)
            def _(zs=zs):
                remote(w_all.at[zs], w_all.at[zs], own_sem.at[0], w_recv.at[zs], me).wait_recv()

            copies.start(there & (above if up else below), functools.partial(weight, zs, False, up))

    for t in range(1, depth):
        pass_on(t)
        pass_weight(t - 1)
        pass_across(t - 1)
    pass_across(depth - 1)
    pass_weight(depth - 1)
    for zs in range(depth):
        arrived(1, zs * PLANE + px)
        arrived(0, zs * PLANE + py)
        arrived(0, zs * PLANE + pd)
        arrived(1, zs * PLANE + pd)
    for copy in locals_:
        copy.wait()
    copies.finish()


def gather(depth, half, keys, values, weight):
    blocks = depth * PLANE
    dma = pltpu.SemaphoreType.DMA
    anywhere = pl.BlockSpec(memory_space=pl.ANY)
    return pl.pallas_call(
        functools.partial(gather_kernel, depth, half),
        out_shape=(
            jax.ShapeDtypeStruct((blocks,) + keys.shape, keys.dtype),
            jax.ShapeDtypeStruct((blocks,) + values.shape, values.dtype),
            jax.ShapeDtypeStruct((depth, half, weight.shape[1]), weight.dtype),
        ),
        in_specs=[anywhere] * 3,
        out_specs=(anywhere,) * 3,
        scratch_shapes=[
            dma((3,)), dma((2, depth, 2)), dma((2, depth, 2)), dma((2, depth)),
            dma((2, blocks)), dma((depth, 2)), dma((depth,)),
        ],
        compiler_params=pltpu.CompilerParams(
            collective_id=0, has_side_effects=True, vmem_limit_bytes=vmem_limit
        ),
    )(keys, values, weight)


def project_kernel(depth, half, hid_ref, w_ref, w_first, out_ref,
                   hid, w_late, theirs, mine_half, other_half, final, landed,
                   own_sem, hid_send, relay_send, hid_recv, w_send, w_recv,
                   core_send, core_recv, out_send, out_recv):
    z, p, px, py, pd = place_of(depth)
    me = z * PLANE + p
    core = lax.axis_index("head")
    rows = hid_ref.shape[0]
    cols = w_ref.shape[1]
    share = depth // 2
    barrier = pltpu.get_barrier_semaphore()
    greeted = (
        z * PLANE + px, z * PLANE + py, z * PLANE + pd,
        (z + 1) % depth * PLANE + p, (z + depth - 1) % depth * PLANE + p,
    )
    for other in greeted:
        pl.semaphore_signal(barrier, inc=1, device_id={"ctx": other}, device_id_type=MESH)
    pl.semaphore_signal(barrier, inc=1, device_id={"head": 1 - core}, device_id_type=MESH)
    pl.semaphore_wait(barrier, len(greeted) + 1)

    copies = Copies()
    always = z >= 0
    above = z + 1 < depth
    below = z > 0
    own_parts = [hid_ref.at[:, pl.ds(s * half, half)] for s in range(2)]
    w_own = w_ref.at[pl.ds(half, half), :]

    def send_hidden(part, axis):
        target = z * PLANE + (px if axis == 0 else py)
        return remote(own_parts[part], hid.at[p, part], hid_send.at[part, axis], hid_recv.at[p, part], target)

    def relay_hidden(part):
        source, target = (px, py) if part == 0 else (py, px)
        slot = hid.at[source, part]
        return remote(slot, slot, relay_send.at[part], hid_recv.at[source, part], z * PLANE + target)

    def hidden_arrived(source, part):
        slot = hid.at[source, part]
        remote(slot, slot, own_sem.at[0], hid_recv.at[source, part], me).wait_recv()

    def weight(zs, own, up):
        target = (z + 1 if up else z - 1) * PLANE + p
        dst = w_late.at[zs]
        return remote(w_own if own else dst, dst, w_send.at[zs, int(up)], w_recv.at[zs], target)

    for part in range(2):
        copies.start(always, functools.partial(send_hidden, part, part))
    copies.start(above, functools.partial(weight, z, True, True))
    copies.start(below, functools.partial(weight, z, True, False))
    for part in range(2):
        copies.start(always, functools.partial(send_hidden, part, 1 - part))
    locals_ = [pltpu.make_async_copy(own_parts[s], hid.at[p, s], own_sem.at[s]) for s in range(2)]
    locals_.append(pltpu.make_async_copy(w_own, w_late.at[z], own_sem.at[2]))
    for copy in locals_:
        copy.start()

    def pass_weight(t):
        for up in (True, False):
            zs = z - t if up else z + t
            there = z >= t if up else zs < depth

            @pl.when(there)
            def _(zs=zs):
                remote(w_late.at[zs], w_late.at[zs], own_sem.at[0], w_recv.at[zs], me).wait_recv()

            copies.start(there & (above if up else below), functools.partial(weight, zs, False, up))

    for t in range(1, depth):
        pass_weight(t)
        if t == 1:
            for part in range(2):
                hidden_arrived(px if part == 0 else py, part)
                copies.start(always, functools.partial(relay_hidden, part))
    for copy in locals_:
        copy.wait()

    def term(source, chunk):
        return (
            jnp.dot(hid[source, 0], w_first[chunk], preferred_element_type=jnp.float32)
            + jnp.dot(hid[source, 1], w_late[chunk], preferred_element_type=jnp.float32)
        ).astype(jnp.bfloat16)

    def core_copy(slot):
        return pltpu.make_async_remote_copy(
            src_ref=other_half.at[slot], dst_ref=theirs.at[slot],
            send_sem=core_send.at[slot], recv_sem=core_recv.at[slot],
            device_id={"head": 1 - core}, device_id_type=MESH,
        )

    def finished(slot, target):
        return remote(final.at[slot], landed.at[p], out_send.at[slot], out_recv.at[p], z * PLANE + target)

    order = (p, px, py, pd)

    def settle(slot):
        core_copy(slot).wait_recv()
        summed = (
            mine_half[slot].astype(jnp.float32) + theirs[slot].astype(jnp.float32)
        ).astype(jnp.bfloat16)
        if slot == 0:
            landed[p] = summed
        else:
            final[slot] = summed
            copies.start(always, functools.partial(finished, slot, order[slot]))

    for slot, source in enumerate(order):
        if slot in (1, 2):
            hidden_arrived(source, 2 - slot)
        if slot == 3:
            hidden_arrived(source, 0)
            hidden_arrived(source, 1)
        for j in range(share):
            other_half[slot, j] = term(source, (1 - core) * share + j)
        core_copy(slot).start()
        for j in range(share):
            mine_half[slot, j] = term(source, core * share + j)
        if slot:
            settle(slot - 1)
    settle(PLANE - 1)
    for slot in range(1, PLANE):
        source = order[slot]
        remote(landed.at[source], landed.at[source], own_sem.at[0], out_recv.at[source], me).wait_recv()
    for source in range(PLANE):
        for j in range(share):
            at = (j * PLANE + source) * cols
            out_ref[:, at:at + cols] = landed[source, j]
    for slot in range(PLANE):
        core_copy(slot).wait_send()
    copies.finish()


def project(depth, half, hidden, weight, w_first):
    rows, width = hidden.shape
    cols = weight.shape[1]
    share = depth // 2
    dma = pltpu.SemaphoreType.DMA
    vmem = pl.BlockSpec(memory_space=pltpu.VMEM)
    block = pltpu.VMEM((PLANE, share, rows, cols), jnp.bfloat16)
    return pl.pallas_call(
        functools.partial(project_kernel, depth, half),
        out_shape=jax.ShapeDtypeStruct((rows, share * PLANE * cols), hidden.dtype),
        in_specs=[vmem] * 3,
        out_specs=vmem,
        scratch_shapes=[
            pltpu.VMEM((PLANE, 2, rows, half), jnp.bfloat16),
            pltpu.VMEM((depth, half, cols), jnp.bfloat16),
            block, block, block, block, block,
            dma((3,)), dma((2, 2)), dma((2,)), dma((PLANE, 2)), dma((depth, 2)), dma((depth,)),
            dma((PLANE,)), dma((PLANE,)), dma((PLANE,)), dma((PLANE,)),
        ],
        compiler_params=pltpu.CompilerParams(
            collective_id=1, has_side_effects=True, vmem_limit_bytes=vmem_limit
        ),
    )(hidden, weight, w_first)


def body(fast, placement, queries, keys, values, weight):
    blocks = placement.shape[0]
    depth = blocks // PLANE
    half = weight.shape[0] // 2
    table = jnp.arange(blocks, dtype=jnp.int32)
    own_block = jnp.sum(jnp.where(table == lax.axis_index("ctx"), placement, 0))[None]
    if fast:
        all_keys, all_values, w_first = gather(depth, half, keys, values, weight)
    else:
        all_keys = lax.all_gather(keys, "ctx", axis=0)
        all_values = lax.all_gather(values, "ctx", axis=0)
    hidden = attend(placement, own_block, queries, all_keys, all_values)
    if fast:
        return project(depth, half, hidden, weight, w_first)
    partial_sum = jnp.dot(
        hidden,
        lax.all_gather(weight, "ctx", axis=1, tiled=True),
        preferred_element_type=jnp.float32,
    )
    term = lax.optimization_barrier(partial_sum.astype(jnp.bfloat16))
    return lax.psum_scatter(term, "head", scatter_dimension=1, tiled=True)


def solution(mesh):
    placed = (P(), P("ctx", "head"), P("ctx", "head"), P("ctx", "head"), P("head", "ctx"))
    fast = mesh.shape["head"] == 2 and mesh.shape["ctx"] == 4 * PLANE
    return jax.shard_map(
        functools.partial(body, fast), mesh=mesh, in_specs=placed,
        out_specs=P("ctx", "head"), check_vma=False,
    )
```

```python
import functools

import jax
import jax.numpy as jnp
from jax import lax
from jax.experimental import pallas as pl
from jax.experimental.pallas import tpu as pltpu
from jax.sharding import PartitionSpec as P

HEAD_FEATURES = 128
PLANE = 4
LOG2_E = 1.4426950408889634
MESH = pl.DeviceIdType.MESH
lowest = -1e30
vmem_limit = 60 * 1024 * 1024


def attend_kernel(scale, place_ref, own_ref, q_ref, k_ref, v_ref, o_ref, stacked, peak, total, acc):
    blocks, rows, _ = k_ref.shape
    heads = q_ref.shape[1] // HEAD_FEATURES
    for i in range(heads):
        stacked[i * rows:(i + 1) * rows, :] = q_ref[:, i * HEAD_FEATURES:(i + 1) * HEAD_FEATURES]
    peak[...] = jnp.full_like(peak, lowest)
    total[...] = jnp.zeros_like(total)
    acc[...] = jnp.zeros_like(acc)
    mine = own_ref[0]

    def update(j, diagonal):
        keys = k_ref[j]
        values = v_ref[j]
        for i in range(heads):
            cols = slice(i * rows, (i + 1) * rows)
            scores = lax.dot_general(
                keys, stacked[cols, :], (((1,), (1,)), ((), ())), preferred_element_type=jnp.float32
            )
            if diagonal:
                key_at = lax.broadcasted_iota(jnp.int32, scores.shape, 0)
                query_at = lax.broadcasted_iota(jnp.int32, scores.shape, 1)
                scores = jnp.where(key_at <= query_at, scores, lowest)
            old = peak[:, cols]
            new = jnp.maximum(old, jnp.max(scores, axis=0, keepdims=True))
            weights = jnp.exp2((scores - new) * scale)
            shrink = jnp.exp2((old - new) * scale)
            peak[:, cols] = new
            total[:, cols] = total[:, cols] * shrink + jnp.sum(weights, axis=0, keepdims=True)
            acc[:, cols] = acc[:, cols] * shrink + lax.dot_general(
                values, weights.astype(jnp.bfloat16), (((0,), (0,)), ((), ())),
                preferred_element_type=jnp.float32,
            )

    def step(j, carry):
        at = place_ref[j]

        @pl.when(at < mine)
        def _():
            update(j, False)

        @pl.when(at == mine)
        def _():
            update(j, True)

        return carry

    lax.fori_loop(0, blocks, step, 0)
    for i in range(heads):
        cols = slice(i * rows, (i + 1) * rows)
        out = acc[:, cols] / total[:, cols]
        o_ref[:, i * HEAD_FEATURES:(i + 1) * HEAD_FEATURES] = out.T.astype(o_ref.dtype)


def attend(placement, own_block, queries, keys, values):
    blocks, rows, width = keys.shape
    kv_heads = width // HEAD_FEATURES
    group = queries.shape[1] // kv_heads
    common = group // HEAD_FEATURES
    scale = HEAD_FEATURES ** (-0.5) * LOG2_E
    return pl.pallas_call(
        functools.partial(attend_kernel, scale),
        out_shape=jax.ShapeDtypeStruct(queries.shape, queries.dtype),
        grid_spec=pltpu.PrefetchScalarGridSpec(
            num_scalar_prefetch=2,
            grid=(kv_heads,),
            in_specs=[
                pl.BlockSpec((rows, group), lambda g, *_: (0, g)),
                pl.BlockSpec((blocks, rows, HEAD_FEATURES), lambda g, *_: (0, 0, g)),
                pl.BlockSpec((blocks, rows, HEAD_FEATURES), lambda g, *_: (0, 0, g)),
            ],
            out_specs=pl.BlockSpec((rows, group), lambda g, *_: (0, g)),
            scratch_shapes=[
                pltpu.VMEM((common * rows, HEAD_FEATURES), jnp.bfloat16),
                pltpu.VMEM((1, common * rows), jnp.float32),
                pltpu.VMEM((1, common * rows), jnp.float32),
                pltpu.VMEM((HEAD_FEATURES, common * rows), jnp.float32),
            ],
        ),
        compiler_params=pltpu.CompilerParams(vmem_limit_bytes=vmem_limit),
        cost_estimate=pl.CostEstimate(
            flops=4 * blocks * rows * rows * queries.shape[1],
            bytes_accessed=4 * (keys.size + queries.size),
            transcendentals=blocks * rows * rows * kv_heads * common,
        ),
    )(placement, own_block, queries, keys, values)


def place_of(depth):
    me = lax.axis_index("ctx")
    z = me // PLANE
    p = me % PLANE
    flip_x = p + 1 - 2 * (p % 2)
    flip_y = (p + 2) % PLANE
    return z, p, flip_x, flip_y, (flip_x + 2) % PLANE


class Copies:
    def __init__(self):
        self.started = []

    def start(self, condition, make):
        @pl.when(condition)
        def _():
            make().start()

        self.started.append((condition, make))

    def finish(self):
        for condition, make in self.started:
            @pl.when(condition)
            def _(make=make):
                make().wait_send()


def remote(src, dst, send, recv, target):
    return pltpu.make_async_remote_copy(
        src_ref=src, dst_ref=dst, send_sem=send, recv_sem=recv,
        device_id={"ctx": target}, device_id_type=MESH,
    )


def gather_attend_kernel(depth, half, scale, place_ref, q_ref, k_ref, v_ref, w_ref, o_ref, w_all,
                         k_all, v_all, turned, peak, total, acc,
                         own_sem, line_send, plane_send, relay_send, recv, w_send, w_recv):
    z, p, px, py, pd = place_of(depth)
    me = z * PLANE + p
    barrier = pltpu.get_barrier_semaphore()
    greeted = (
        z * PLANE + px, z * PLANE + py,
        (z + 1) % depth * PLANE + p, (z + depth - 1) % depth * PLANE + p,
    )
    for other in greeted:
        pl.semaphore_signal(barrier, inc=1, device_id={"ctx": other}, device_id_type=MESH)
    pl.semaphore_wait(barrier, len(greeted))

    w_own = w_ref.at[pl.ds(0, half), :]
    w_local = pltpu.make_async_copy(w_own, w_all.at[z], own_sem.at[0])
    copies = Copies()
    pairs = ((k_ref, k_all), (v_ref, v_all))

    def arrived(array, source):
        ref = pairs[array][1].at[source]
        remote(ref, ref, own_sem.at[0], recv.at[array, source], me).wait_recv()

    def move(array, source, own, send, target):
        dst = pairs[array][1].at[source]
        src = pairs[array][0] if own else dst
        return remote(src, dst, send, recv.at[array, source], target)

    def line(array, zs, own, up):
        target = (z + 1 if up else z - 1) * PLANE + p
        return move(array, zs * PLANE + p, own, line_send.at[array, zs, int(up)], target)

    def plane(array, zs, own, axis):
        target = z * PLANE + (px if axis == 0 else py)
        return move(array, zs * PLANE + p, own, plane_send.at[array, zs, axis], target)

    def relay(array, zs):
        source, target = (px, py) if array == 0 else (py, px)
        return move(array, zs * PLANE + source, False, relay_send.at[array, zs], z * PLANE + target)

    def weight(zs, own, up):
        target = (z + 1 if up else z - 1) * PLANE + p
        dst = w_all.at[zs]
        return remote(w_own if own else dst, dst, w_send.at[zs, int(up)], w_recv.at[zs], target)

    above = z + 1 < depth
    below = z > 0
    always = z >= 0
    reach = {}
    for t in range(depth):
        reach[t, True] = z - t, z >= t, (z >= t) & above
        reach[t, False] = z + t, z + t < depth, (z + t < depth) & below
    for array in range(2):
        copies.start(above, functools.partial(line, array, z, True, True))
        copies.start(below, functools.partial(line, array, z, True, False))
    for array in range(2):
        for axis in range(2):
            copies.start(always, functools.partial(plane, array, z, True, axis))
    w_local.start()

    def pass_on(t):
        for up in (True, False):
            zs, there, on = reach[t, up]

            @pl.when(there)
            def _(zs=zs):
                for array in range(2):
                    arrived(array, zs * PLANE + p)

            for array in range(2):
                copies.start(on, functools.partial(line, array, zs, False, up))
            for array in range(2):
                for axis in range(2):
                    copies.start(there, functools.partial(plane, array, zs, False, axis))

    def pass_across(t):
        for up in (True, False)[: 1 if t == 0 else 2]:
            zs, there, on = reach[t, up]

            @pl.when(there)
            def _(zs=zs):
                arrived(0, zs * PLANE + px)
                arrived(1, zs * PLANE + py)

            for array in range(2):
                copies.start(there, functools.partial(relay, array, zs))

    def pass_weight(t):
        if t == 0:
            copies.start(above, functools.partial(weight, z, True, True))
            copies.start(below, functools.partial(weight, z, True, False))
            return
        for up in (True, False):
            zs, there, on = reach[t, up]

            @pl.when(there)
            def _(zs=zs):
                remote(w_all.at[zs], w_all.at[zs], own_sem.at[0], w_recv.at[zs], me).wait_recv()

            copies.start(on, functools.partial(weight, zs, False, up))

    rows = q_ref.shape[0]
    heads = q_ref.shape[1] // HEAD_FEATURES
    common = q_ref.shape[1] // k_ref.shape[1]

    def features(h):
        return slice(h * HEAD_FEATURES, (h + 1) * HEAD_FEATURES)

    for h in range(heads):
        turned[h] = q_ref[:, features(h)].T

    def update(read_keys, read_values, bias, first):
        def score(h):
            return jnp.dot(
                read_keys(features(h // common)), turned[h], preferred_element_type=jnp.float32
            )

        following = score(0)
        for h in range(heads):
            scores = following
            if h + 1 < heads:
                following = score(h + 1)
            if h % common == 0:
                values = read_values(features(h // common)).T
            if first:
                key_at = lax.broadcasted_iota(jnp.int32, scores.shape, 0)
                query_at = lax.broadcasted_iota(jnp.int32, scores.shape, 1)
                scores = jnp.where(key_at <= query_at, scores, lowest)
                new = jnp.max(scores, axis=0, keepdims=True)
                weights = jnp.exp2((scores - new) * scale)
            else:
                old = peak[h]
                new = jnp.maximum(old, jnp.max(scores, axis=0, keepdims=True) + bias)
                weights = jnp.exp2((scores - (new - bias)) * scale)
                shrink = jnp.exp2((old - new) * scale)
            sums = jnp.sum(weights, axis=0, keepdims=True)
            part = jnp.dot(values, weights.astype(jnp.bfloat16), preferred_element_type=jnp.float32)
            peak[h] = new
            if first:
                total[h] = sums
                acc[h] = part
            else:
                total[h] = total[h] * shrink + sums
                acc[h] = acc[h] * shrink + part

    update(lambda f: k_ref[:, f], lambda f: v_ref[:, f], 0.0, True)
    pass_on(1)
    pass_weight(0)
    pass_across(0)

    near = z - 1 + 2 * ((depth - 1 - z) // (depth - 1))
    last = (depth - 1) * (1 - z // 2)
    third = depth * (depth - 1) // 2 - z - near - last
    services = {
        3: ((pass_on, 2),),
        4: ((pass_across, 1), (pass_weight, 1)),
        6: ((pass_on, 3),),
        8: ((pass_across, 2), (pass_weight, 2)),
        12: ((pass_across, 3), (pass_weight, 3)),
    }

    def step(n, carry):
        for at, calls in services.items():
            @pl.when(n == at)
            def _(calls=calls):
                for call, t in calls:
                    call(t)

        r = n // PLANE
        s = n % PLANE
        zs = jnp.where(r == 0, z, jnp.where(r == 1, near, jnp.where(r == 2, third, last)))
        source = zs * PLANE + (p // 2 + s // 2) % 2 * 2 + (p % 2 + s % 2) % 2

        @pl.when(s == 1)
        def _():
            arrived(1, source)

        @pl.when(s == 2)
        def _():
            arrived(0, source)

        @pl.when(s == 3)
        def _():
            arrived(0, source)
            arrived(1, source)

        bias = jnp.where(place_ref[source] < place_ref[me], 0.0, lowest)
        update(
            lambda f: k_all[source, :, f], lambda f: v_all[source, :, f], bias, False
        )
        return carry

    lax.fori_loop(1, depth * PLANE, step, 0)
    for h in range(heads):
        o_ref[:, features(h)] = (acc[h] / total[h]).T.astype(o_ref.dtype)
    w_local.wait()
    copies.finish()


def gather_attend(depth, half, placement, queries, keys, values, weight):
    blocks = depth * PLANE
    rows = queries.shape[0]
    heads = queries.shape[1] // HEAD_FEATURES
    scale = HEAD_FEATURES ** (-0.5) * LOG2_E
    dma = pltpu.SemaphoreType.DMA
    anywhere = pl.BlockSpec(memory_space=pl.ANY)
    vmem = pl.BlockSpec(memory_space=pltpu.VMEM)
    return pl.pallas_call(
        functools.partial(gather_attend_kernel, depth, half, scale),
        out_shape=(
            jax.ShapeDtypeStruct(queries.shape, queries.dtype),
            jax.ShapeDtypeStruct((depth, half, weight.shape[1]), weight.dtype),
        ),
        in_specs=[pl.BlockSpec(memory_space=pltpu.SMEM), vmem, vmem, vmem, anywhere],
        out_specs=(vmem, anywhere),
        scratch_shapes=[
            pltpu.VMEM((blocks,) + keys.shape, keys.dtype),
            pltpu.VMEM((blocks,) + values.shape, values.dtype),
            pltpu.VMEM((heads, HEAD_FEATURES, rows), queries.dtype),
            pltpu.VMEM((heads, 1, rows), jnp.float32),
            pltpu.VMEM((heads, 1, rows), jnp.float32),
            pltpu.VMEM((heads, HEAD_FEATURES, rows), jnp.float32),
            dma((1,)), dma((2, depth, 2)), dma((2, depth, 2)), dma((2, depth)),
            dma((2, blocks)), dma((depth, 2)), dma((depth,)),
        ],
        compiler_params=pltpu.CompilerParams(
            collective_id=0, has_side_effects=True, vmem_limit_bytes=vmem_limit
        ),
    )(placement, queries, keys, values, weight)


def project_kernel(depth, half, hid_ref, w_ref, w_first, out_ref,
                   hid, w_late, theirs, mine_half, other_half, final, landed,
                   own_sem, hid_send, relay_send, hid_recv, w_send, w_recv,
                   core_send, core_recv, out_send, out_recv):
    z, p, px, py, pd = place_of(depth)
    me = z * PLANE + p
    core = lax.axis_index("head")
    rows = hid_ref.shape[0]
    cols = w_ref.shape[1]
    share = depth // 2
    barrier = pltpu.get_barrier_semaphore()
    greeted = (
        z * PLANE + px, z * PLANE + py, z * PLANE + pd,
        (z + 1) % depth * PLANE + p, (z + depth - 1) % depth * PLANE + p,
    )
    for other in greeted:
        pl.semaphore_signal(barrier, inc=1, device_id={"ctx": other}, device_id_type=MESH)
    pl.semaphore_signal(barrier, inc=1, device_id={"head": 1 - core}, device_id_type=MESH)
    pl.semaphore_wait(barrier, len(greeted) + 1)

    copies = Copies()
    always = z >= 0
    above = z + 1 < depth
    below = z > 0
    own_parts = [hid_ref.at[:, pl.ds(s * half, half)] for s in range(2)]
    w_own = w_ref.at[pl.ds(half, half), :]

    def send_hidden(part, axis):
        target = z * PLANE + (px if axis == 0 else py)
        return remote(own_parts[part], hid.at[p, part], hid_send.at[part, axis], hid_recv.at[p, part], target)

    def relay_hidden(part):
        source, target = (px, py) if part == 0 else (py, px)
        slot = hid.at[source, part]
        return remote(slot, slot, relay_send.at[part], hid_recv.at[source, part], z * PLANE + target)

    def hidden_arrived(source, part):
        slot = hid.at[source, part]
        remote(slot, slot, own_sem.at[0], hid_recv.at[source, part], me).wait_recv()

    def weight(zs, own, up):
        target = (z + 1 if up else z - 1) * PLANE + p
        dst = w_late.at[zs]
        return remote(w_own if own else dst, dst, w_send.at[zs, int(up)], w_recv.at[zs], target)

    for part in range(2):
        copies.start(always, functools.partial(send_hidden, part, part))
    copies.start(above, functools.partial(weight, z, True, True))
    copies.start(below, functools.partial(weight, z, True, False))
    for part in range(2):
        copies.start(always, functools.partial(send_hidden, part, 1 - part))
    locals_ = [pltpu.make_async_copy(own_parts[s], hid.at[p, s], own_sem.at[s]) for s in range(2)]
    locals_.append(pltpu.make_async_copy(w_own, w_late.at[z], own_sem.at[2]))
    for copy in locals_:
        copy.start()

    def pass_weight(t):
        for up in (True, False):
            zs = z - t if up else z + t
            there = z >= t if up else zs < depth

            @pl.when(there)
            def _(zs=zs):
                remote(w_late.at[zs], w_late.at[zs], own_sem.at[0], w_recv.at[zs], me).wait_recv()

            copies.start(there & (above if up else below), functools.partial(weight, zs, False, up))

    for t in range(1, depth):
        pass_weight(t)
        if t == 1:
            for part in range(2):
                hidden_arrived(px if part == 0 else py, part)
                copies.start(always, functools.partial(relay_hidden, part))
    for copy in locals_:
        copy.wait()

    def term(source, chunk):
        return (
            jnp.dot(hid[source, 0], w_first[chunk], preferred_element_type=jnp.float32)
            + jnp.dot(hid[source, 1], w_late[chunk], preferred_element_type=jnp.float32)
        ).astype(jnp.bfloat16)

    def core_copy(slot):
        return pltpu.make_async_remote_copy(
            src_ref=other_half.at[slot], dst_ref=theirs.at[slot],
            send_sem=core_send.at[slot], recv_sem=core_recv.at[slot],
            device_id={"head": 1 - core}, device_id_type=MESH,
        )

    def finished(slot, target):
        return remote(final.at[slot], landed.at[p], out_send.at[slot], out_recv.at[p], z * PLANE + target)

    order = (p, px, py, pd)

    def settle(slot):
        core_copy(slot).wait_recv()
        summed = (
            mine_half[slot].astype(jnp.float32) + theirs[slot].astype(jnp.float32)
        ).astype(jnp.bfloat16)
        if slot == 0:
            landed[p] = summed
        else:
            final[slot] = summed
            copies.start(always, functools.partial(finished, slot, order[slot]))

    for slot, source in enumerate(order):
        if slot in (1, 2):
            hidden_arrived(source, 2 - slot)
        if slot == 3:
            hidden_arrived(source, 0)
            hidden_arrived(source, 1)
        for j in range(share):
            other_half[slot, j] = term(source, (1 - core) * share + j)
        core_copy(slot).start()
        for j in range(share):
            mine_half[slot, j] = term(source, core * share + j)
        if slot:
            settle(slot - 1)
    settle(PLANE - 1)
    for slot in range(1, PLANE):
        source = order[slot]
        remote(landed.at[source], landed.at[source], own_sem.at[0], out_recv.at[source], me).wait_recv()
    for source in range(PLANE):
        for j in range(share):
            at = (j * PLANE + source) * cols
            out_ref[:, at:at + cols] = landed[source, j]
    for slot in range(PLANE):
        core_copy(slot).wait_send()
    copies.finish()


def project(depth, half, hidden, weight, w_first):
    rows, width = hidden.shape
    cols = weight.shape[1]
    share = depth // 2
    dma = pltpu.SemaphoreType.DMA
    vmem = pl.BlockSpec(memory_space=pltpu.VMEM)
    block = pltpu.VMEM((PLANE, share, rows, cols), jnp.bfloat16)
    return pl.pallas_call(
        functools.partial(project_kernel, depth, half),
        out_shape=jax.ShapeDtypeStruct((rows, share * PLANE * cols), hidden.dtype),
        in_specs=[vmem] * 3,
        out_specs=vmem,
        scratch_shapes=[
            pltpu.VMEM((PLANE, 2, rows, half), jnp.bfloat16),
            pltpu.VMEM((depth, half, cols), jnp.bfloat16),
            block, block, block, block, block,
            dma((3,)), dma((2, 2)), dma((2,)), dma((PLANE, 2)), dma((depth, 2)), dma((depth,)),
            dma((PLANE,)), dma((PLANE,)), dma((PLANE,)), dma((PLANE,)),
        ],
        compiler_params=pltpu.CompilerParams(
            collective_id=1, has_side_effects=True, vmem_limit_bytes=vmem_limit
        ),
    )(hidden, weight, w_first)


def body(fast, placement, queries, keys, values, weight):
    blocks = placement.shape[0]
    depth = blocks // PLANE
    half = weight.shape[0] // 2
    table = jnp.arange(blocks, dtype=jnp.int32)
    own_block = jnp.sum(jnp.where(table == lax.axis_index("ctx"), placement, 0))[None]
    if fast:
        hidden, w_first = gather_attend(depth, half, placement, queries, keys, values, weight)
        return project(depth, half, hidden, weight, w_first)
    all_keys = lax.all_gather(keys, "ctx", axis=0)
    all_values = lax.all_gather(values, "ctx", axis=0)
    hidden = attend(placement, own_block, queries, all_keys, all_values)
    partial_sum = jnp.dot(
        hidden,
        lax.all_gather(weight, "ctx", axis=1, tiled=True),
        preferred_element_type=jnp.float32,
    )
    term = lax.optimization_barrier(partial_sum.astype(jnp.bfloat16))
    return lax.psum_scatter(term, "head", scatter_dimension=1, tiled=True)


def solution(mesh):
    placed = (P(), P("ctx", "head"), P("ctx", "head"), P("ctx", "head"), P("head", "ctx"))
    fast = mesh.shape["head"] == 2 and mesh.shape["ctx"] == 4 * PLANE
    return jax.shard_map(
        functools.partial(body, fast), mesh=mesh, in_specs=placed,
        out_specs=P("ctx", "head"), check_vma=False,
    )
```

```python
import functools

import jax
import jax.numpy as jnp
from jax import lax
from jax.experimental import pallas as pl
from jax.experimental.pallas import tpu as pltpu
from jax.sharding import PartitionSpec as P

HEAD_FEATURES = 128
PLANE = 4
LOG2_E = 1.4426950408889634
MESH = pl.DeviceIdType.MESH
lowest = -1e30
vmem_limit = 60 * 1024 * 1024


def attend_kernel(scale, place_ref, own_ref, q_ref, k_ref, v_ref, o_ref, stacked, peak, total, acc):
    blocks, rows, _ = k_ref.shape
    heads = q_ref.shape[1] // HEAD_FEATURES
    for i in range(heads):
        stacked[i * rows:(i + 1) * rows, :] = q_ref[:, i * HEAD_FEATURES:(i + 1) * HEAD_FEATURES]
    peak[...] = jnp.full_like(peak, lowest)
    total[...] = jnp.zeros_like(total)
    acc[...] = jnp.zeros_like(acc)
    mine = own_ref[0]

    def update(j, diagonal):
        keys = k_ref[j]
        values = v_ref[j]
        for i in range(heads):
            cols = slice(i * rows, (i + 1) * rows)
            scores = lax.dot_general(
                keys, stacked[cols, :], (((1,), (1,)), ((), ())), preferred_element_type=jnp.float32
            )
            if diagonal:
                key_at = lax.broadcasted_iota(jnp.int32, scores.shape, 0)
                query_at = lax.broadcasted_iota(jnp.int32, scores.shape, 1)
                scores = jnp.where(key_at <= query_at, scores, lowest)
            old = peak[:, cols]
            new = jnp.maximum(old, jnp.max(scores, axis=0, keepdims=True))
            weights = jnp.exp2((scores - new) * scale)
            shrink = jnp.exp2((old - new) * scale)
            peak[:, cols] = new
            total[:, cols] = total[:, cols] * shrink + jnp.sum(weights, axis=0, keepdims=True)
            acc[:, cols] = acc[:, cols] * shrink + lax.dot_general(
                values, weights.astype(jnp.bfloat16), (((0,), (0,)), ((), ())),
                preferred_element_type=jnp.float32,
            )

    def step(j, carry):
        at = place_ref[j]

        @pl.when(at < mine)
        def _():
            update(j, False)

        @pl.when(at == mine)
        def _():
            update(j, True)

        return carry

    lax.fori_loop(0, blocks, step, 0)
    for i in range(heads):
        cols = slice(i * rows, (i + 1) * rows)
        out = acc[:, cols] / total[:, cols]
        o_ref[:, i * HEAD_FEATURES:(i + 1) * HEAD_FEATURES] = out.T.astype(o_ref.dtype)


def attend(placement, own_block, queries, keys, values):
    blocks, rows, width = keys.shape
    kv_heads = width // HEAD_FEATURES
    group = queries.shape[1] // kv_heads
    common = group // HEAD_FEATURES
    scale = HEAD_FEATURES ** (-0.5) * LOG2_E
    return pl.pallas_call(
        functools.partial(attend_kernel, scale),
        out_shape=jax.ShapeDtypeStruct(queries.shape, queries.dtype),
        grid_spec=pltpu.PrefetchScalarGridSpec(
            num_scalar_prefetch=2,
            grid=(kv_heads,),
            in_specs=[
                pl.BlockSpec((rows, group), lambda g, *_: (0, g)),
                pl.BlockSpec((blocks, rows, HEAD_FEATURES), lambda g, *_: (0, 0, g)),
                pl.BlockSpec((blocks, rows, HEAD_FEATURES), lambda g, *_: (0, 0, g)),
            ],
            out_specs=pl.BlockSpec((rows, group), lambda g, *_: (0, g)),
            scratch_shapes=[
                pltpu.VMEM((common * rows, HEAD_FEATURES), jnp.bfloat16),
                pltpu.VMEM((1, common * rows), jnp.float32),
                pltpu.VMEM((1, common * rows), jnp.float32),
                pltpu.VMEM((HEAD_FEATURES, common * rows), jnp.float32),
            ],
        ),
        compiler_params=pltpu.CompilerParams(vmem_limit_bytes=vmem_limit),
        cost_estimate=pl.CostEstimate(
            flops=4 * blocks * rows * rows * queries.shape[1],
            bytes_accessed=4 * (keys.size + queries.size),
            transcendentals=blocks * rows * rows * kv_heads * common,
        ),
    )(placement, own_block, queries, keys, values)


def place_of(depth):
    me = lax.axis_index("ctx")
    z = me // PLANE
    p = me % PLANE
    flip_x = p + 1 - 2 * (p % 2)
    flip_y = (p + 2) % PLANE
    return z, p, flip_x, flip_y, (flip_x + 2) % PLANE


class Copies:
    def __init__(self):
        self.started = []

    def start(self, condition, make):
        @pl.when(condition)
        def _():
            make().start()

        self.started.append((condition, make))

    def finish(self):
        for condition, make in self.started:
            @pl.when(condition)
            def _(make=make):
                make().wait_send()


def remote(src, dst, send, recv, target):
    return pltpu.make_async_remote_copy(
        src_ref=src, dst_ref=dst, send_sem=send, recv_sem=recv,
        device_id={"ctx": target}, device_id_type=MESH,
    )


def gather_attend_kernel(depth, early, scale, place_ref, q_ref, k_ref, v_ref, w_ref, o_ref, w_all,
                         k_all, v_all, turned, peak, total, acc,
                         own_sem, line_send, plane_send, relay_send, recv, w_send, w_recv):
    z, p, px, py, pd = place_of(depth)
    me = z * PLANE + p
    barrier = pltpu.get_barrier_semaphore()
    greeted = (
        z * PLANE + px, z * PLANE + py,
        (z + 1) % depth * PLANE + p, (z + depth - 1) % depth * PLANE + p,
    )
    for other in greeted:
        pl.semaphore_signal(barrier, inc=1, device_id={"ctx": other}, device_id_type=MESH)
    pl.semaphore_wait(barrier, len(greeted))

    w_own = w_ref.at[pl.ds(0, early), :]
    w_local = pltpu.make_async_copy(w_own, w_all.at[z], own_sem.at[0])
    copies = Copies()
    pairs = ((k_ref, k_all), (v_ref, v_all))

    def arrived(array, source):
        ref = pairs[array][1].at[source]
        remote(ref, ref, own_sem.at[0], recv.at[array, source], me).wait_recv()

    def move(array, source, own, send, target):
        dst = pairs[array][1].at[source]
        src = pairs[array][0] if own else dst
        return remote(src, dst, send, recv.at[array, source], target)

    def line(array, zs, own, up):
        target = (z + 1 if up else z - 1) * PLANE + p
        return move(array, zs * PLANE + p, own, line_send.at[array, zs, int(up)], target)

    def plane(array, zs, own, axis):
        target = z * PLANE + (px if axis == 0 else py)
        return move(array, zs * PLANE + p, own, plane_send.at[array, zs, axis], target)

    def relay(array, zs):
        source, target = (px, py) if array == 0 else (py, px)
        return move(array, zs * PLANE + source, False, relay_send.at[array, zs], z * PLANE + target)

    def weight(zs, own, up):
        target = (z + 1 if up else z - 1) * PLANE + p
        dst = w_all.at[zs]
        return remote(w_own if own else dst, dst, w_send.at[zs, int(up)], w_recv.at[zs], target)

    above = z + 1 < depth
    below = z > 0
    always = z >= 0
    reach = {}
    for t in range(depth):
        reach[t, True] = z - t, z >= t, (z >= t) & above
        reach[t, False] = z + t, z + t < depth, (z + t < depth) & below
    for array in range(2):
        copies.start(above, functools.partial(line, array, z, True, True))
        copies.start(below, functools.partial(line, array, z, True, False))
    for array in range(2):
        for axis in range(2):
            copies.start(always, functools.partial(plane, array, z, True, axis))
    w_local.start()

    def pass_on(t):
        for up in (True, False):
            zs, there, on = reach[t, up]

            @pl.when(there)
            def _(zs=zs):
                for array in range(2):
                    arrived(array, zs * PLANE + p)

            for array in range(2):
                copies.start(on, functools.partial(line, array, zs, False, up))
            for array in range(2):
                for axis in range(2):
                    copies.start(there, functools.partial(plane, array, zs, False, axis))

    def pass_across(t):
        for up in (True, False)[: 1 if t == 0 else 2]:
            zs, there, on = reach[t, up]

            @pl.when(there)
            def _(zs=zs):
                arrived(0, zs * PLANE + px)
                arrived(1, zs * PLANE + py)

            for array in range(2):
                copies.start(there, functools.partial(relay, array, zs))

    def pass_weight(t):
        if t == 0:
            copies.start(above, functools.partial(weight, z, True, True))
            copies.start(below, functools.partial(weight, z, True, False))
            return
        for up in (True, False):
            zs, there, on = reach[t, up]

            @pl.when(there)
            def _(zs=zs):
                remote(w_all.at[zs], w_all.at[zs], own_sem.at[0], w_recv.at[zs], me).wait_recv()

            copies.start(on, functools.partial(weight, zs, False, up))

    rows = q_ref.shape[0]
    heads = q_ref.shape[1] // HEAD_FEATURES
    common = q_ref.shape[1] // k_ref.shape[1]

    def features(h):
        return slice(h * HEAD_FEATURES, (h + 1) * HEAD_FEATURES)

    for h in range(heads):
        at = h % common * rows
        turned[h // common, :, at:at + rows] = q_ref[:, features(h)].T

    def update(read_keys, read_values, bias, first):
        def score(g):
            return jnp.dot(read_keys(features(g)), turned[g], preferred_element_type=jnp.float32)

        following = score(0)
        for g in range(heads // common):
            scores = following
            if g + 1 < heads // common:
                following = score(g + 1)
            values = read_values(features(g)).T
            if first:
                key_at = lax.broadcasted_iota(jnp.int32, scores.shape, 0)
                query_at = lax.broadcasted_iota(jnp.int32, scores.shape, 1) % rows
                scores = jnp.where(key_at <= query_at, scores, lowest)
                new = jnp.max(scores, axis=0, keepdims=True)
                weights = jnp.exp2((scores - new) * scale)
            else:
                old = peak[g]
                new = jnp.maximum(old, jnp.max(scores, axis=0, keepdims=True) + bias)
                weights = jnp.exp2((scores - (new - bias)) * scale)
                shrink = jnp.exp2((old - new) * scale)
            sums = jnp.sum(weights, axis=0, keepdims=True)
            part = jnp.dot(values, weights.astype(jnp.bfloat16), preferred_element_type=jnp.float32)
            peak[g] = new
            if first:
                total[g] = sums
                acc[g] = part
            else:
                total[g] = total[g] * shrink + sums
                acc[g] = acc[g] * shrink + part

    update(lambda f: k_ref[:, f], lambda f: v_ref[:, f], 0.0, True)
    pass_on(1)
    pass_weight(0)
    pass_across(0)

    near = z - 1 + 2 * ((depth - 1 - z) // (depth - 1))
    last = (depth - 1) * (1 - z // 2)
    third = depth * (depth - 1) // 2 - z - near - last
    services = {
        3: ((pass_on, 2),),
        4: ((pass_across, 1), (pass_weight, 1)),
        6: ((pass_on, 3),),
        8: ((pass_across, 2), (pass_weight, 2)),
        12: ((pass_across, 3), (pass_weight, 3)),
    }

    def step(n, carry):
        for at, calls in services.items():
            @pl.when(n == at)
            def _(calls=calls):
                for call, t in calls:
                    call(t)

        r = n // PLANE
        s = n % PLANE
        zs = jnp.where(r == 0, z, jnp.where(r == 1, near, jnp.where(r == 2, third, last)))
        source = zs * PLANE + (p // 2 + s // 2) % 2 * 2 + (p % 2 + s % 2) % 2

        @pl.when(s == 1)
        def _():
            arrived(1, source)

        @pl.when(s == 2)
        def _():
            arrived(0, source)

        @pl.when(s == 3)
        def _():
            arrived(0, source)
            arrived(1, source)

        bias = jnp.where(place_ref[source] < place_ref[me], 0.0, lowest)
        update(
            lambda f: k_all[source, :, f], lambda f: v_all[source, :, f], bias, False
        )
        return carry

    lax.fori_loop(1, depth * PLANE, step, 0)
    for h in range(heads):
        cols = slice(h % common * rows, (h % common + 1) * rows)
        out = acc[h // common, :, cols] / total[h // common, :, cols]
        o_ref[:, features(h)] = out.T.astype(o_ref.dtype)
    w_local.wait()
    copies.finish()


def gather_attend(depth, early, placement, queries, keys, values, weight):
    blocks = depth * PLANE
    rows = queries.shape[0]
    groups = keys.shape[1] // HEAD_FEATURES
    lanes = rows * queries.shape[1] // keys.shape[1]
    scale = HEAD_FEATURES ** (-0.5) * LOG2_E
    dma = pltpu.SemaphoreType.DMA
    anywhere = pl.BlockSpec(memory_space=pl.ANY)
    vmem = pl.BlockSpec(memory_space=pltpu.VMEM)
    return pl.pallas_call(
        functools.partial(gather_attend_kernel, depth, early, scale),
        out_shape=(
            jax.ShapeDtypeStruct(queries.shape, queries.dtype),
            jax.ShapeDtypeStruct((depth, early, weight.shape[1]), weight.dtype),
        ),
        in_specs=[pl.BlockSpec(memory_space=pltpu.SMEM), vmem, vmem, vmem, anywhere],
        out_specs=(vmem, anywhere),
        scratch_shapes=[
            pltpu.VMEM((blocks,) + keys.shape, keys.dtype),
            pltpu.VMEM((blocks,) + values.shape, values.dtype),
            pltpu.VMEM((groups, HEAD_FEATURES, lanes), queries.dtype),
            pltpu.VMEM((groups, 1, lanes), jnp.float32),
            pltpu.VMEM((groups, 1, lanes), jnp.float32),
            pltpu.VMEM((groups, HEAD_FEATURES, lanes), jnp.float32),
            dma((1,)), dma((2, depth, 2)), dma((2, depth, 2)), dma((2, depth)),
            dma((2, blocks)), dma((depth, 2)), dma((depth,)),
        ],
        compiler_params=pltpu.CompilerParams(
            collective_id=0, has_side_effects=True, vmem_limit_bytes=vmem_limit
        ),
    )(placement, queries, keys, values, weight)


def project_kernel(depth, half, hid_ref, w_ref, w_first, out_ref,
                   hid, w_late, theirs, mine_half, other_half, final, landed,
                   own_sem, hid_send, relay_send, hid_recv, w_send, w_recv,
                   core_send, core_recv, out_send, out_recv):
    z, p, px, py, pd = place_of(depth)
    me = z * PLANE + p
    core = lax.axis_index("head")
    rows = hid_ref.shape[0]
    cols = w_ref.shape[1]
    share = depth // 2
    barrier = pltpu.get_barrier_semaphore()
    greeted = (
        z * PLANE + px, z * PLANE + py, z * PLANE + pd,
        (z + 1) % depth * PLANE + p, (z + depth - 1) % depth * PLANE + p,
    )
    for other in greeted:
        pl.semaphore_signal(barrier, inc=1, device_id={"ctx": other}, device_id_type=MESH)
    pl.semaphore_signal(barrier, inc=1, device_id={"head": 1 - core}, device_id_type=MESH)
    pl.semaphore_wait(barrier, len(greeted) + 1)

    copies = Copies()
    always = z >= 0
    above = z + 1 < depth
    below = z > 0
    own_parts = [hid_ref.at[:, pl.ds(s * half, half)] for s in range(2)]
    early = w_first.shape[1]
    w_own = w_ref.at[pl.ds(early, 2 * half - early), :]

    def send_hidden(part, axis):
        target = z * PLANE + (px if axis == 0 else py)
        return remote(own_parts[part], hid.at[p, part], hid_send.at[part, axis], hid_recv.at[p, part], target)

    def relay_hidden(part):
        source, target = (px, py) if part == 0 else (py, px)
        slot = hid.at[source, part]
        return remote(slot, slot, relay_send.at[part], hid_recv.at[source, part], z * PLANE + target)

    def hidden_arrived(source, part):
        slot = hid.at[source, part]
        remote(slot, slot, own_sem.at[0], hid_recv.at[source, part], me).wait_recv()

    def weight(zs, own, up):
        target = (z + 1 if up else z - 1) * PLANE + p
        dst = w_late.at[zs]
        return remote(w_own if own else dst, dst, w_send.at[zs, int(up)], w_recv.at[zs], target)

    for part in range(2):
        copies.start(always, functools.partial(send_hidden, part, part))
    copies.start(above, functools.partial(weight, z, True, True))
    copies.start(below, functools.partial(weight, z, True, False))
    for part in range(2):
        copies.start(always, functools.partial(send_hidden, part, 1 - part))
    locals_ = [pltpu.make_async_copy(own_parts[s], hid.at[p, s], own_sem.at[s]) for s in range(2)]
    locals_.append(pltpu.make_async_copy(w_own, w_late.at[z], own_sem.at[2]))
    for copy in locals_:
        copy.start()

    def pass_weight(t):
        for up in (True, False):
            zs = z - t if up else z + t
            there = z >= t if up else zs < depth

            @pl.when(there)
            def _(zs=zs):
                remote(w_late.at[zs], w_late.at[zs], own_sem.at[0], w_recv.at[zs], me).wait_recv()

            copies.start(there & (above if up else below), functools.partial(weight, zs, False, up))

    for t in range(1, depth):
        pass_weight(t)
        if t == 2:
            for part in range(2):
                hidden_arrived(px if part == 0 else py, part)
                copies.start(always, functools.partial(relay_hidden, part))
    for copy in locals_:
        copy.wait()

    def term(source, chunk):
        return (
            jnp.dot(hid[source, 0], w_first[chunk, :half], preferred_element_type=jnp.float32)
            + jnp.dot(
                hid[source, 1, :, :early - half], w_first[chunk, half:],
                preferred_element_type=jnp.float32,
            )
            + jnp.dot(
                hid[source, 1, :, early - half:], w_late[chunk],
                preferred_element_type=jnp.float32,
            )
        ).astype(jnp.bfloat16)

    def core_copy(slot):
        return pltpu.make_async_remote_copy(
            src_ref=other_half.at[slot], dst_ref=theirs.at[slot],
            send_sem=core_send.at[slot], recv_sem=core_recv.at[slot],
            device_id={"head": 1 - core}, device_id_type=MESH,
        )

    def finished(slot, target):
        return remote(final.at[slot], landed.at[p], out_send.at[slot], out_recv.at[p], z * PLANE + target)

    order = (p, px, py, pd)

    def settle(slot):
        core_copy(slot).wait_recv()
        summed = (
            mine_half[slot].astype(jnp.float32) + theirs[slot].astype(jnp.float32)
        ).astype(jnp.bfloat16)
        if slot == 0:
            landed[p] = summed
        else:
            final[slot] = summed
            copies.start(always, functools.partial(finished, slot, order[slot]))

    for slot, source in enumerate(order):
        if slot in (1, 2):
            hidden_arrived(source, 2 - slot)
        if slot == 3:
            hidden_arrived(source, 0)
            hidden_arrived(source, 1)
        for j in range(share):
            other_half[slot, j] = term(source, (1 - core) * share + j)
        core_copy(slot).start()
        for j in range(share):
            mine_half[slot, j] = term(source, core * share + j)
        if slot:
            settle(slot - 1)
    settle(PLANE - 1)
    for slot in range(1, PLANE):
        source = order[slot]
        remote(landed.at[source], landed.at[source], own_sem.at[0], out_recv.at[source], me).wait_recv()
    for source in range(PLANE):
        for j in range(share):
            at = (j * PLANE + source) * cols
            out_ref[:, at:at + cols] = landed[source, j]
    for slot in range(PLANE):
        core_copy(slot).wait_send()
    copies.finish()


def project(depth, half, hidden, weight, w_first):
    rows, width = hidden.shape
    cols = weight.shape[1]
    share = depth // 2
    dma = pltpu.SemaphoreType.DMA
    vmem = pl.BlockSpec(memory_space=pltpu.VMEM)
    block = pltpu.VMEM((PLANE, share, rows, cols), jnp.bfloat16)
    return pl.pallas_call(
        functools.partial(project_kernel, depth, half),
        out_shape=jax.ShapeDtypeStruct((rows, share * PLANE * cols), hidden.dtype),
        in_specs=[vmem] * 3,
        out_specs=vmem,
        scratch_shapes=[
            pltpu.VMEM((PLANE, 2, rows, half), jnp.bfloat16),
            pltpu.VMEM((depth, 2 * half - w_first.shape[1], cols), jnp.bfloat16),
            block, block, block, block, block,
            dma((3,)), dma((2, 2)), dma((2,)), dma((PLANE, 2)), dma((depth, 2)), dma((depth,)),
            dma((PLANE,)), dma((PLANE,)), dma((PLANE,)), dma((PLANE,)),
        ],
        compiler_params=pltpu.CompilerParams(
            collective_id=1, has_side_effects=True, vmem_limit_bytes=vmem_limit
        ),
    )(hidden, weight, w_first)


def body(fast, placement, queries, keys, values, weight):
    blocks = placement.shape[0]
    depth = blocks // PLANE
    half = weight.shape[0] // 2
    early = half + half // 2
    table = jnp.arange(blocks, dtype=jnp.int32)
    own_block = jnp.sum(jnp.where(table == lax.axis_index("ctx"), placement, 0))[None]
    if fast:
        hidden, w_first = gather_attend(depth, early, placement, queries, keys, values, weight)
        return project(depth, half, hidden, weight, w_first)
    all_keys = lax.all_gather(keys, "ctx", axis=0)
    all_values = lax.all_gather(values, "ctx", axis=0)
    hidden = attend(placement, own_block, queries, all_keys, all_values)
    partial_sum = jnp.dot(
        hidden,
        lax.all_gather(weight, "ctx", axis=1, tiled=True),
        preferred_element_type=jnp.float32,
    )
    term = lax.optimization_barrier(partial_sum.astype(jnp.bfloat16))
    return lax.psum_scatter(term, "head", scatter_dimension=1, tiled=True)


def solution(mesh):
    placed = (P(), P("ctx", "head"), P("ctx", "head"), P("ctx", "head"), P("head", "ctx"))
    fast = mesh.shape["head"] == 2 and mesh.shape["ctx"] == 4 * PLANE
    return jax.shard_map(
        functools.partial(body, fast), mesh=mesh, in_specs=placed,
        out_specs=P("ctx", "head"), check_vma=False,
    )
```

```python
import functools

import jax
import jax.numpy as jnp
from jax import lax
from jax.experimental import pallas as pl
from jax.experimental.pallas import tpu as pltpu
from jax.sharding import PartitionSpec as P

HEAD_FEATURES = 128
PLANE = 4
LOG2_E = 1.4426950408889634
MESH = pl.DeviceIdType.MESH
lowest = -1e30
vmem_limit = 60 * 1024 * 1024


def attend_kernel(scale, place_ref, own_ref, q_ref, k_ref, v_ref, o_ref, stacked, peak, total, acc):
    blocks, rows, _ = k_ref.shape
    heads = q_ref.shape[1] // HEAD_FEATURES
    for i in range(heads):
        stacked[i * rows:(i + 1) * rows, :] = q_ref[:, i * HEAD_FEATURES:(i + 1) * HEAD_FEATURES]
    peak[...] = jnp.full_like(peak, lowest)
    total[...] = jnp.zeros_like(total)
    acc[...] = jnp.zeros_like(acc)
    mine = own_ref[0]

    def update(j, diagonal):
        keys = k_ref[j]
        values = v_ref[j]
        for i in range(heads):
            cols = slice(i * rows, (i + 1) * rows)
            scores = lax.dot_general(
                keys, stacked[cols, :], (((1,), (1,)), ((), ())), preferred_element_type=jnp.float32
            )
            if diagonal:
                key_at = lax.broadcasted_iota(jnp.int32, scores.shape, 0)
                query_at = lax.broadcasted_iota(jnp.int32, scores.shape, 1)
                scores = jnp.where(key_at <= query_at, scores, lowest)
            old = peak[:, cols]
            new = jnp.maximum(old, jnp.max(scores, axis=0, keepdims=True))
            weights = jnp.exp2((scores - new) * scale)
            shrink = jnp.exp2((old - new) * scale)
            peak[:, cols] = new
            total[:, cols] = total[:, cols] * shrink + jnp.sum(weights, axis=0, keepdims=True)
            acc[:, cols] = acc[:, cols] * shrink + lax.dot_general(
                values, weights.astype(jnp.bfloat16), (((0,), (0,)), ((), ())),
                preferred_element_type=jnp.float32,
            )

    def step(j, carry):
        at = place_ref[j]

        @pl.when(at < mine)
        def _():
            update(j, False)

        @pl.when(at == mine)
        def _():
            update(j, True)

        return carry

    lax.fori_loop(0, blocks, step, 0)
    for i in range(heads):
        cols = slice(i * rows, (i + 1) * rows)
        out = acc[:, cols] / total[:, cols]
        o_ref[:, i * HEAD_FEATURES:(i + 1) * HEAD_FEATURES] = out.T.astype(o_ref.dtype)


def attend(placement, own_block, queries, keys, values):
    blocks, rows, width = keys.shape
    kv_heads = width // HEAD_FEATURES
    group = queries.shape[1] // kv_heads
    common = group // HEAD_FEATURES
    scale = HEAD_FEATURES ** (-0.5) * LOG2_E
    return pl.pallas_call(
        functools.partial(attend_kernel, scale),
        out_shape=jax.ShapeDtypeStruct(queries.shape, queries.dtype),
        grid_spec=pltpu.PrefetchScalarGridSpec(
            num_scalar_prefetch=2,
            grid=(kv_heads,),
            in_specs=[
                pl.BlockSpec((rows, group), lambda g, *_: (0, g)),
                pl.BlockSpec((blocks, rows, HEAD_FEATURES), lambda g, *_: (0, 0, g)),
                pl.BlockSpec((blocks, rows, HEAD_FEATURES), lambda g, *_: (0, 0, g)),
            ],
            out_specs=pl.BlockSpec((rows, group), lambda g, *_: (0, g)),
            scratch_shapes=[
                pltpu.VMEM((common * rows, HEAD_FEATURES), jnp.bfloat16),
                pltpu.VMEM((1, common * rows), jnp.float32),
                pltpu.VMEM((1, common * rows), jnp.float32),
                pltpu.VMEM((HEAD_FEATURES, common * rows), jnp.float32),
            ],
        ),
        compiler_params=pltpu.CompilerParams(vmem_limit_bytes=vmem_limit),
        cost_estimate=pl.CostEstimate(
            flops=4 * blocks * rows * rows * queries.shape[1],
            bytes_accessed=4 * (keys.size + queries.size),
            transcendentals=blocks * rows * rows * kv_heads * common,
        ),
    )(placement, own_block, queries, keys, values)


def place_of(depth):
    me = lax.axis_index("ctx")
    z = me // PLANE
    p = me % PLANE
    flip_x = p + 1 - 2 * (p % 2)
    flip_y = (p + 2) % PLANE
    return z, p, flip_x, flip_y, (flip_x + 2) % PLANE


class Copies:
    def __init__(self):
        self.started = []

    def start(self, condition, make):
        @pl.when(condition)
        def _():
            make().start()

        self.started.append((condition, make))

    def finish(self):
        for condition, make in self.started:
            @pl.when(condition)
            def _(make=make):
                make().wait_send()


def remote(src, dst, send, recv, target):
    return pltpu.make_async_remote_copy(
        src_ref=src, dst_ref=dst, send_sem=send, recv_sem=recv,
        device_id={"ctx": target}, device_id_type=MESH,
    )


def gather_attend_kernel(depth, early, scale, place_ref, q_ref, k_ref, v_ref, w_ref, o_ref, w_all,
                         k_all, v_all, turned, peak, acc,
                         own_sem, line_send, plane_send, relay_send, recv, w_send, w_recv):
    z, p, px, py, pd = place_of(depth)
    me = z * PLANE + p
    barrier = pltpu.get_barrier_semaphore()
    greeted = (
        z * PLANE + px, z * PLANE + py,
        (z + 1) % depth * PLANE + p, (z + depth - 1) % depth * PLANE + p,
    )
    for other in greeted:
        pl.semaphore_signal(barrier, inc=1, device_id={"ctx": other}, device_id_type=MESH)
    pl.semaphore_wait(barrier, len(greeted))

    w_own = w_ref.at[pl.ds(0, early), :]
    w_local = pltpu.make_async_copy(w_own, w_all.at[z], own_sem.at[0])
    copies = Copies()
    pairs = ((k_ref, k_all), (v_ref, v_all))

    def arrived(array, source):
        ref = pairs[array][1].at[source]
        remote(ref, ref, own_sem.at[0], recv.at[array, source], me).wait_recv()

    def move(array, source, own, send, target):
        dst = pairs[array][1].at[source]
        src = pairs[array][0] if own else dst
        return remote(src, dst, send, recv.at[array, source], target)

    def line(array, zs, own, up):
        target = (z + 1 if up else z - 1) * PLANE + p
        return move(array, zs * PLANE + p, own, line_send.at[array, zs, int(up)], target)

    def plane(array, zs, own, axis):
        target = z * PLANE + (px if axis == 0 else py)
        return move(array, zs * PLANE + p, own, plane_send.at[array, zs, axis], target)

    def relay(array, zs):
        source, target = (px, py) if array == 0 else (py, px)
        return move(array, zs * PLANE + source, False, relay_send.at[array, zs], z * PLANE + target)

    def weight(zs, own, up):
        target = (z + 1 if up else z - 1) * PLANE + p
        dst = w_all.at[zs]
        return remote(w_own if own else dst, dst, w_send.at[zs, int(up)], w_recv.at[zs], target)

    above = z + 1 < depth
    below = z > 0
    always = z >= 0
    reach = {}
    for t in range(depth):
        reach[t, True] = z - t, z >= t, (z >= t) & above
        reach[t, False] = z + t, z + t < depth, (z + t < depth) & below
    for array in range(2):
        copies.start(above, functools.partial(line, array, z, True, True))
        copies.start(below, functools.partial(line, array, z, True, False))
    for array in range(2):
        for axis in range(2):
            copies.start(always, functools.partial(plane, array, z, True, axis))
    w_local.start()

    def pass_on(t):
        for up in (True, False):
            zs, there, on = reach[t, up]

            @pl.when(there)
            def _(zs=zs):
                for array in range(2):
                    arrived(array, zs * PLANE + p)

            for array in range(2):
                copies.start(on, functools.partial(line, array, zs, False, up))
            for array in range(2):
                for axis in range(2):
                    copies.start(there, functools.partial(plane, array, zs, False, axis))

    def pass_across(t):
        for up in (True, False)[: 1 if t == 0 else 2]:
            zs, there, on = reach[t, up]

            @pl.when(there)
            def _(zs=zs):
                arrived(0, zs * PLANE + px)
                arrived(1, zs * PLANE + py)

            for array in range(2):
                copies.start(there, functools.partial(relay, array, zs))

    def pass_weight(t):
        if t == 0:
            copies.start(above, functools.partial(weight, z, True, True))
            copies.start(below, functools.partial(weight, z, True, False))
            return
        for up in (True, False):
            zs, there, on = reach[t, up]

            @pl.when(there)
            def _(zs=zs):
                remote(w_all.at[zs], w_all.at[zs], own_sem.at[0], w_recv.at[zs], me).wait_recv()

            copies.start(on, functools.partial(weight, zs, False, up))

    rows = q_ref.shape[0]
    heads = q_ref.shape[1] // HEAD_FEATURES
    common = q_ref.shape[1] // k_ref.shape[1]

    def features(h):
        return slice(h * HEAD_FEATURES, (h + 1) * HEAD_FEATURES)

    for h in range(heads):
        at = h % common * rows
        turned[h // common, :, at:at + rows] = q_ref[:, features(h)].T

    ones = jnp.ones((16, rows), v_ref.dtype)

    def update(read_keys, read_values, bias, first):
        def score(g):
            return jnp.dot(read_keys(features(g)), turned[g], preferred_element_type=jnp.float32)

        following = score(0)
        for g in range(heads // common):
            scores = following
            if g + 1 < heads // common:
                following = score(g + 1)
            values = jnp.concatenate([read_values(features(g)).T, ones], axis=0)
            if first:
                key_at = lax.broadcasted_iota(jnp.int32, scores.shape, 0)
                query_at = lax.broadcasted_iota(jnp.int32, scores.shape, 1) % rows
                scores = jnp.where(key_at <= query_at, scores, lowest)
                new = jnp.max(scores, axis=0, keepdims=True)
                weights = jnp.exp2((scores - new) * scale)
            else:
                old = peak[g]
                new = jnp.maximum(old, jnp.max(scores, axis=0, keepdims=True) + bias)
                weights = jnp.exp2((scores - (new - bias)) * scale)
                shrink = jnp.exp2((old - new) * scale)
            part = jnp.dot(values, weights.astype(jnp.bfloat16), preferred_element_type=jnp.float32)
            peak[g] = new
            if first:
                acc[g] = part
            else:
                acc[g] = acc[g] * shrink + part

    update(lambda f: k_ref[:, f], lambda f: v_ref[:, f], 0.0, True)
    pass_on(1)
    pass_weight(0)
    pass_across(0)

    near = z - 1 + 2 * ((depth - 1 - z) // (depth - 1))
    last = (depth - 1) * (1 - z // 2)
    third = depth * (depth - 1) // 2 - z - near - last
    services = {
        3: ((pass_on, 2),),
        4: ((pass_across, 1), (pass_weight, 1)),
        6: ((pass_on, 3),),
        8: ((pass_across, 2), (pass_weight, 2)),
        12: ((pass_across, 3), (pass_weight, 3)),
    }

    def step(n, carry):
        for at, calls in services.items():
            @pl.when(n == at)
            def _(calls=calls):
                for call, t in calls:
                    call(t)

        r = n // PLANE
        s = n % PLANE
        zs = jnp.where(r == 0, z, jnp.where(r == 1, near, jnp.where(r == 2, third, last)))
        source = zs * PLANE + (p // 2 + s // 2) % 2 * 2 + (p % 2 + s % 2) % 2

        @pl.when(s == 1)
        def _():
            arrived(1, source)

        @pl.when(s == 2)
        def _():
            arrived(0, source)

        @pl.when(s == 3)
        def _():
            arrived(0, source)
            arrived(1, source)

        bias = jnp.where(place_ref[source] < place_ref[me], 0.0, lowest)
        update(
            lambda f: k_all[source, :, f], lambda f: v_all[source, :, f], bias, False
        )
        return carry

    lax.fori_loop(1, depth * PLANE, step, 0)
    for h in range(heads):
        cols = slice(h % common * rows, (h % common + 1) * rows)
        total = acc[h // common, HEAD_FEATURES:HEAD_FEATURES + 1, cols]
        out = acc[h // common, :HEAD_FEATURES, cols] / total
        o_ref[:, features(h)] = out.T.astype(o_ref.dtype)
    w_local.wait()
    copies.finish()


def gather_attend(depth, early, placement, queries, keys, values, weight):
    blocks = depth * PLANE
    rows = queries.shape[0]
    groups = keys.shape[1] // HEAD_FEATURES
    lanes = rows * queries.shape[1] // keys.shape[1]
    scale = HEAD_FEATURES ** (-0.5) * LOG2_E
    dma = pltpu.SemaphoreType.DMA
    anywhere = pl.BlockSpec(memory_space=pl.ANY)
    vmem = pl.BlockSpec(memory_space=pltpu.VMEM)
    return pl.pallas_call(
        functools.partial(gather_attend_kernel, depth, early, scale),
        out_shape=(
            jax.ShapeDtypeStruct(queries.shape, queries.dtype),
            jax.ShapeDtypeStruct((depth, early, weight.shape[1]), weight.dtype),
        ),
        in_specs=[pl.BlockSpec(memory_space=pltpu.SMEM), vmem, vmem, vmem, anywhere],
        out_specs=(vmem, anywhere),
        scratch_shapes=[
            pltpu.VMEM((blocks,) + keys.shape, keys.dtype),
            pltpu.VMEM((blocks,) + values.shape, values.dtype),
            pltpu.VMEM((groups, HEAD_FEATURES, lanes), queries.dtype),
            pltpu.VMEM((groups, 1, lanes), jnp.float32),
            pltpu.VMEM((groups, HEAD_FEATURES + 16, lanes), jnp.float32),
            dma((1,)), dma((2, depth, 2)), dma((2, depth, 2)), dma((2, depth)),
            dma((2, blocks)), dma((depth, 2)), dma((depth,)),
        ],
        compiler_params=pltpu.CompilerParams(
            collective_id=0, has_side_effects=True, vmem_limit_bytes=vmem_limit
        ),
    )(placement, queries, keys, values, weight)


def project_kernel(depth, half, hid_ref, w_ref, w_first, out_ref,
                   hid, w_late, theirs, mine_half, other_half, final, landed,
                   own_sem, hid_send, relay_send, hid_recv, w_send, w_recv,
                   core_send, core_recv, out_send, out_recv):
    z, p, px, py, pd = place_of(depth)
    me = z * PLANE + p
    core = lax.axis_index("head")
    rows = hid_ref.shape[0]
    cols = w_ref.shape[1]
    share = depth // 2
    barrier = pltpu.get_barrier_semaphore()
    greeted = (
        z * PLANE + px, z * PLANE + py, z * PLANE + pd,
        (z + 1) % depth * PLANE + p, (z + depth - 1) % depth * PLANE + p,
    )
    for other in greeted:
        pl.semaphore_signal(barrier, inc=1, device_id={"ctx": other}, device_id_type=MESH)
    pl.semaphore_signal(barrier, inc=1, device_id={"head": 1 - core}, device_id_type=MESH)
    pl.semaphore_wait(barrier, len(greeted) + 1)

    copies = Copies()
    always = z >= 0
    above = z + 1 < depth
    below = z > 0
    own_parts = [hid_ref.at[:, pl.ds(s * half, half)] for s in range(2)]
    early = w_first.shape[1]
    w_own = w_ref.at[pl.ds(early, 2 * half - early), :]

    def send_hidden(part, axis):
        target = z * PLANE + (px if axis == 0 else py)
        return remote(own_parts[part], hid.at[p, part], hid_send.at[part, axis], hid_recv.at[p, part], target)

    def relay_hidden(part):
        source, target = (px, py) if part == 0 else (py, px)
        slot = hid.at[source, part]
        return remote(slot, slot, relay_send.at[part], hid_recv.at[source, part], z * PLANE + target)

    def hidden_arrived(source, part):
        slot = hid.at[source, part]
        remote(slot, slot, own_sem.at[0], hid_recv.at[source, part], me).wait_recv()

    def weight(zs, own, up):
        target = (z + 1 if up else z - 1) * PLANE + p
        dst = w_late.at[zs]
        return remote(w_own if own else dst, dst, w_send.at[zs, int(up)], w_recv.at[zs], target)

    for part in range(2):
        copies.start(always, functools.partial(send_hidden, part, part))
    copies.start(above, functools.partial(weight, z, True, True))
    copies.start(below, functools.partial(weight, z, True, False))
    for part in range(2):
        copies.start(always, functools.partial(send_hidden, part, 1 - part))
    locals_ = [pltpu.make_async_copy(own_parts[s], hid.at[p, s], own_sem.at[s]) for s in range(2)]
    locals_.append(pltpu.make_async_copy(w_own, w_late.at[z], own_sem.at[2]))
    for copy in locals_:
        copy.start()

    def pass_weight(t):
        for up in (True, False):
            zs = z - t if up else z + t
            there = z >= t if up else zs < depth

            @pl.when(there)
            def _(zs=zs):
                remote(w_late.at[zs], w_late.at[zs], own_sem.at[0], w_recv.at[zs], me).wait_recv()

            copies.start(there & (above if up else below), functools.partial(weight, zs, False, up))

    for t in range(1, depth):
        pass_weight(t)
        if t == 1:
            for part in range(2):
                hidden_arrived(px if part == 0 else py, part)
                copies.start(always, functools.partial(relay_hidden, part))
    for copy in locals_:
        copy.wait()

    def term(source, chunk):
        return (
            jnp.dot(hid[source, 0], w_first[chunk, :half], preferred_element_type=jnp.float32)
            + jnp.dot(
                hid[source, 1, :, :early - half], w_first[chunk, half:],
                preferred_element_type=jnp.float32,
            )
            + jnp.dot(
                hid[source, 1, :, early - half:], w_late[chunk],
                preferred_element_type=jnp.float32,
            )
        ).astype(jnp.bfloat16)

    def core_copy(slot):
        return pltpu.make_async_remote_copy(
            src_ref=other_half.at[slot], dst_ref=theirs.at[slot],
            send_sem=core_send.at[slot], recv_sem=core_recv.at[slot],
            device_id={"head": 1 - core}, device_id_type=MESH,
        )

    def finished(slot, target):
        return remote(final.at[slot], landed.at[p], out_send.at[slot], out_recv.at[p], z * PLANE + target)

    order = (p, px, py, pd)

    def settle(slot):
        core_copy(slot).wait_recv()
        summed = (
            mine_half[slot].astype(jnp.float32) + theirs[slot].astype(jnp.float32)
        ).astype(jnp.bfloat16)
        if slot == 0:
            landed[p] = summed
        else:
            final[slot] = summed
            copies.start(always, functools.partial(finished, slot, order[slot]))

    for slot, source in enumerate(order):
        if slot in (1, 2):
            hidden_arrived(source, 2 - slot)
        if slot == 3:
            hidden_arrived(source, 0)
            hidden_arrived(source, 1)
        for j in range(share):
            other_half[slot, j] = term(source, (1 - core) * share + j)
        core_copy(slot).start()
        for j in range(share):
            mine_half[slot, j] = term(source, core * share + j)
        if slot:
            settle(slot - 1)
    settle(PLANE - 1)
    for slot in range(1, PLANE):
        source = order[slot]
        remote(landed.at[source], landed.at[source], own_sem.at[0], out_recv.at[source], me).wait_recv()
    for source in range(PLANE):
        for j in range(share):
            at = (j * PLANE + source) * cols
            out_ref[:, at:at + cols] = landed[source, j]
    for slot in range(PLANE):
        core_copy(slot).wait_send()
    copies.finish()


def project(depth, half, hidden, weight, w_first):
    rows, width = hidden.shape
    cols = weight.shape[1]
    share = depth // 2
    dma = pltpu.SemaphoreType.DMA
    vmem = pl.BlockSpec(memory_space=pltpu.VMEM)
    block = pltpu.VMEM((PLANE, share, rows, cols), jnp.bfloat16)
    return pl.pallas_call(
        functools.partial(project_kernel, depth, half),
        out_shape=jax.ShapeDtypeStruct((rows, share * PLANE * cols), hidden.dtype),
        in_specs=[vmem] * 3,
        out_specs=vmem,
        scratch_shapes=[
            pltpu.VMEM((PLANE, 2, rows, half), jnp.bfloat16),
            pltpu.VMEM((depth, 2 * half - w_first.shape[1], cols), jnp.bfloat16),
            block, block, block, block, block,
            dma((3,)), dma((2, 2)), dma((2,)), dma((PLANE, 2)), dma((depth, 2)), dma((depth,)),
            dma((PLANE,)), dma((PLANE,)), dma((PLANE,)), dma((PLANE,)),
        ],
        compiler_params=pltpu.CompilerParams(
            collective_id=1, has_side_effects=True, vmem_limit_bytes=vmem_limit
        ),
    )(hidden, weight, w_first)


def body(fast, placement, queries, keys, values, weight):
    blocks = placement.shape[0]
    depth = blocks // PLANE
    half = weight.shape[0] // 2
    early = half + half // 4
    table = jnp.arange(blocks, dtype=jnp.int32)
    own_block = jnp.sum(jnp.where(table == lax.axis_index("ctx"), placement, 0))[None]
    if fast:
        hidden, w_first = gather_attend(depth, early, placement, queries, keys, values, weight)
        return project(depth, half, hidden, weight, w_first)
    all_keys = lax.all_gather(keys, "ctx", axis=0)
    all_values = lax.all_gather(values, "ctx", axis=0)
    hidden = attend(placement, own_block, queries, all_keys, all_values)
    partial_sum = jnp.dot(
        hidden,
        lax.all_gather(weight, "ctx", axis=1, tiled=True),
        preferred_element_type=jnp.float32,
    )
    term = lax.optimization_barrier(partial_sum.astype(jnp.bfloat16))
    return lax.psum_scatter(term, "head", scatter_dimension=1, tiled=True)


def solution(mesh):
    placed = (P(), P("ctx", "head"), P("ctx", "head"), P("ctx", "head"), P("head", "ctx"))
    fast = mesh.shape["head"] == 2 and mesh.shape["ctx"] == 4 * PLANE
    return jax.shard_map(
        functools.partial(body, fast), mesh=mesh, in_specs=placed,
        out_specs=P("ctx", "head"), check_vma=False,
    )
```

```python
import functools

import jax
import jax.numpy as jnp
from jax import lax
from jax.experimental import pallas as pl
from jax.experimental.pallas import tpu as pltpu
from jax.sharding import PartitionSpec as P

HEAD_FEATURES = 128
PLANE = 4
LOG2_E = 1.4426950408889634
MESH = pl.DeviceIdType.MESH
lowest = -1e30
vmem_limit = 60 * 1024 * 1024


def attend_kernel(scale, place_ref, own_ref, q_ref, k_ref, v_ref, o_ref, stacked, peak, total, acc):
    blocks, rows, _ = k_ref.shape
    heads = q_ref.shape[1] // HEAD_FEATURES
    for i in range(heads):
        stacked[i * rows:(i + 1) * rows, :] = q_ref[:, i * HEAD_FEATURES:(i + 1) * HEAD_FEATURES]
    peak[...] = jnp.full_like(peak, lowest)
    total[...] = jnp.zeros_like(total)
    acc[...] = jnp.zeros_like(acc)
    mine = own_ref[0]

    def update(j, diagonal):
        keys = k_ref[j]
        values = v_ref[j]
        for i in range(heads):
            cols = slice(i * rows, (i + 1) * rows)
            scores = lax.dot_general(
                keys, stacked[cols, :], (((1,), (1,)), ((), ())), preferred_element_type=jnp.float32
            )
            if diagonal:
                key_at = lax.broadcasted_iota(jnp.int32, scores.shape, 0)
                query_at = lax.broadcasted_iota(jnp.int32, scores.shape, 1)
                scores = jnp.where(key_at <= query_at, scores, lowest)
            old = peak[:, cols]
            new = jnp.maximum(old, jnp.max(scores, axis=0, keepdims=True))
            weights = jnp.exp2((scores - new) * scale)
            shrink = jnp.exp2((old - new) * scale)
            peak[:, cols] = new
            total[:, cols] = total[:, cols] * shrink + jnp.sum(weights, axis=0, keepdims=True)
            acc[:, cols] = acc[:, cols] * shrink + lax.dot_general(
                values, weights.astype(jnp.bfloat16), (((0,), (0,)), ((), ())),
                preferred_element_type=jnp.float32,
            )

    def step(j, carry):
        at = place_ref[j]

        @pl.when(at < mine)
        def _():
            update(j, False)

        @pl.when(at == mine)
        def _():
            update(j, True)

        return carry

    lax.fori_loop(0, blocks, step, 0)
    for i in range(heads):
        cols = slice(i * rows, (i + 1) * rows)
        out = acc[:, cols] / total[:, cols]
        o_ref[:, i * HEAD_FEATURES:(i + 1) * HEAD_FEATURES] = out.T.astype(o_ref.dtype)


def attend(placement, own_block, queries, keys, values):
    blocks, rows, width = keys.shape
    kv_heads = width // HEAD_FEATURES
    group = queries.shape[1] // kv_heads
    common = group // HEAD_FEATURES
    scale = HEAD_FEATURES ** (-0.5) * LOG2_E
    return pl.pallas_call(
        functools.partial(attend_kernel, scale),
        out_shape=jax.ShapeDtypeStruct(queries.shape, queries.dtype),
        grid_spec=pltpu.PrefetchScalarGridSpec(
            num_scalar_prefetch=2,
            grid=(kv_heads,),
            in_specs=[
                pl.BlockSpec((rows, group), lambda g, *_: (0, g)),
                pl.BlockSpec((blocks, rows, HEAD_FEATURES), lambda g, *_: (0, 0, g)),
                pl.BlockSpec((blocks, rows, HEAD_FEATURES), lambda g, *_: (0, 0, g)),
            ],
            out_specs=pl.BlockSpec((rows, group), lambda g, *_: (0, g)),
            scratch_shapes=[
                pltpu.VMEM((common * rows, HEAD_FEATURES), jnp.bfloat16),
                pltpu.VMEM((1, common * rows), jnp.float32),
                pltpu.VMEM((1, common * rows), jnp.float32),
                pltpu.VMEM((HEAD_FEATURES, common * rows), jnp.float32),
            ],
        ),
        compiler_params=pltpu.CompilerParams(vmem_limit_bytes=vmem_limit),
        cost_estimate=pl.CostEstimate(
            flops=4 * blocks * rows * rows * queries.shape[1],
            bytes_accessed=4 * (keys.size + queries.size),
            transcendentals=blocks * rows * rows * kv_heads * common,
        ),
    )(placement, own_block, queries, keys, values)


def place_of(depth):
    me = lax.axis_index("ctx")
    z = me // PLANE
    p = me % PLANE
    flip_x = p + 1 - 2 * (p % 2)
    flip_y = (p + 2) % PLANE
    return z, p, flip_x, flip_y, (flip_x + 2) % PLANE


class Copies:
    def __init__(self):
        self.started = []

    def start(self, condition, make):
        @pl.when(condition)
        def _():
            make().start()

        self.started.append((condition, make))

    def finish(self):
        for condition, make in self.started:
            @pl.when(condition)
            def _(make=make):
                make().wait_send()


def remote(src, dst, send, recv, target):
    return pltpu.make_async_remote_copy(
        src_ref=src, dst_ref=dst, send_sem=send, recv_sem=recv,
        device_id={"ctx": target}, device_id_type=MESH,
    )


def gather_attend_kernel(depth, early, scale, place_ref, q_ref, k_ref, v_ref, w_ref, o_ref, w_all,
                         k_all, v_all, turned, peak, acc,
                         own_sem, line_send, plane_send, relay_send, recv, w_send, w_recv):
    z, p, px, py, pd = place_of(depth)
    me = z * PLANE + p
    barrier = pltpu.get_barrier_semaphore()
    greeted = (
        z * PLANE + px, z * PLANE + py,
        (z + 1) % depth * PLANE + p, (z + depth - 1) % depth * PLANE + p,
    )
    for other in greeted:
        pl.semaphore_signal(barrier, inc=1, device_id={"ctx": other}, device_id_type=MESH)
    pl.semaphore_wait(barrier, len(greeted))

    w_own = w_ref.at[pl.ds(0, early), :]
    w_local = pltpu.make_async_copy(w_own, w_all.at[z], own_sem.at[0])
    copies = Copies()
    pairs = ((k_ref, k_all), (v_ref, v_all))

    def arrived(array, source):
        ref = pairs[array][1].at[source]
        remote(ref, ref, own_sem.at[0], recv.at[array, source], me).wait_recv()

    def move(array, source, own, send, target):
        dst = pairs[array][1].at[source]
        src = pairs[array][0] if own else dst
        return remote(src, dst, send, recv.at[array, source], target)

    def line(array, zs, own, up):
        target = (z + 1 if up else z - 1) * PLANE + p
        return move(array, zs * PLANE + p, own, line_send.at[array, zs, int(up)], target)

    def plane(array, zs, own, axis):
        target = z * PLANE + (px if axis == 0 else py)
        return move(array, zs * PLANE + p, own, plane_send.at[array, zs, axis], target)

    def relay(array, zs):
        source, target = (px, py) if array == 0 else (py, px)
        return move(array, zs * PLANE + source, False, relay_send.at[array, zs], z * PLANE + target)

    def weight(zs, own, up):
        target = (z + 1 if up else z - 1) * PLANE + p
        dst = w_all.at[zs]
        return remote(w_own if own else dst, dst, w_send.at[zs, int(up)], w_recv.at[zs], target)

    above = z + 1 < depth
    below = z > 0
    always = z >= 0
    reach = {}
    for t in range(depth):
        reach[t, True] = z - t, z >= t, (z >= t) & above
        reach[t, False] = z + t, z + t < depth, (z + t < depth) & below
    for array in range(2):
        copies.start(above, functools.partial(line, array, z, True, True))
        copies.start(below, functools.partial(line, array, z, True, False))
    for array in range(2):
        for axis in range(2):
            copies.start(always, functools.partial(plane, array, z, True, axis))
    w_local.start()

    def pass_on(t):
        for up in (True, False):
            zs, there, on = reach[t, up]

            @pl.when(there)
            def _(zs=zs):
                for array in range(2):
                    arrived(array, zs * PLANE + p)

            for array in range(2):
                copies.start(on, functools.partial(line, array, zs, False, up))
            for array in range(2):
                for axis in range(2):
                    copies.start(there, functools.partial(plane, array, zs, False, axis))

    def pass_across(t):
        for up in (True, False)[: 1 if t == 0 else 2]:
            zs, there, on = reach[t, up]

            @pl.when(there)
            def _(zs=zs):
                arrived(0, zs * PLANE + px)
                arrived(1, zs * PLANE + py)

            for array in range(2):
                copies.start(there, functools.partial(relay, array, zs))

    def pass_weight(t):
        if t == 0:
            copies.start(above, functools.partial(weight, z, True, True))
            copies.start(below, functools.partial(weight, z, True, False))
            return
        for up in (True, False):
            zs, there, on = reach[t, up]

            @pl.when(there)
            def _(zs=zs):
                remote(w_all.at[zs], w_all.at[zs], own_sem.at[0], w_recv.at[zs], me).wait_recv()

            copies.start(on, functools.partial(weight, zs, False, up))

    rows = q_ref.shape[0]
    heads = q_ref.shape[1] // HEAD_FEATURES
    common = q_ref.shape[1] // k_ref.shape[1]

    def features(h):
        return slice(h * HEAD_FEATURES, (h + 1) * HEAD_FEATURES)

    for h in range(heads):
        at = h % common * rows
        turned[h // common, :, at:at + rows] = q_ref[:, features(h)].T

    ones = jnp.ones((16, rows), v_ref.dtype)

    def update(read_keys, read_values, bias, first):
        def score(g):
            return jnp.dot(read_keys(features(g)), turned[g], preferred_element_type=jnp.float32)

        following = score(0)
        for g in range(heads // common):
            scores = following
            if g + 1 < heads // common:
                following = score(g + 1)
            values = jnp.concatenate([read_values(features(g)).T, ones], axis=0)
            if first:
                key_at = lax.broadcasted_iota(jnp.int32, scores.shape, 0)
                query_at = lax.broadcasted_iota(jnp.int32, scores.shape, 1) % rows
                scores = jnp.where(key_at <= query_at, scores, lowest)
                new = jnp.max(scores, axis=0, keepdims=True)
                weights = jnp.exp2((scores - new) * scale)
            else:
                old = peak[g]
                new = jnp.maximum(old, jnp.max(scores, axis=0, keepdims=True) + bias)
                weights = jnp.exp2((scores - (new - bias)) * scale)
                shrink = jnp.exp2((old - new) * scale)
            part = jnp.dot(values, weights.astype(jnp.bfloat16), preferred_element_type=jnp.float32)
            peak[g] = new
            if first:
                acc[g] = part
            else:
                acc[g] = acc[g] * shrink + part

    update(lambda f: k_ref[:, f], lambda f: v_ref[:, f], 0.0, True)
    pass_on(1)
    pass_weight(0)
    pass_across(0)

    near = z - 1 + 2 * ((depth - 1 - z) // (depth - 1))
    last = (depth - 1) * (1 - z // 2)
    third = depth * (depth - 1) // 2 - z - near - last
    services = {
        3: ((pass_on, 2),),
        4: ((pass_across, 1), (pass_weight, 1)),
        6: ((pass_on, 3),),
        8: ((pass_across, 2),),
        9: ((pass_weight, 2),),
        12: ((pass_across, 3),),
    }

    def step(n, carry):
        for at, calls in services.items():
            @pl.when(n == at)
            def _(calls=calls):
                for call, t in calls:
                    call(t)

        r = n // PLANE
        s = n % PLANE
        zs = jnp.where(r == 0, z, jnp.where(r == 1, near, jnp.where(r == 2, third, last)))
        source = zs * PLANE + (p // 2 + s // 2) % 2 * 2 + (p % 2 + s % 2) % 2

        @pl.when(s == 1)
        def _():
            arrived(1, source)

        @pl.when(s == 2)
        def _():
            arrived(0, source)

        @pl.when(s == 3)
        def _():
            arrived(0, source)
            arrived(1, source)

        bias = jnp.where(place_ref[source] < place_ref[me], 0.0, lowest)
        update(
            lambda f: k_all[source, :, f], lambda f: v_all[source, :, f], bias, False
        )
        return carry

    lax.fori_loop(1, depth * PLANE, step, 0)
    for h in range(heads):
        cols = slice(h % common * rows, (h % common + 1) * rows)
        total = acc[h // common, HEAD_FEATURES:HEAD_FEATURES + 1, cols]
        out = acc[h // common, :HEAD_FEATURES, cols] / total
        o_ref[:, features(h)] = out.T.astype(o_ref.dtype)
    pass_weight(3)
    w_local.wait()
    copies.finish()


def gather_attend(depth, early, placement, queries, keys, values, weight):
    blocks = depth * PLANE
    rows = queries.shape[0]
    groups = keys.shape[1] // HEAD_FEATURES
    lanes = rows * queries.shape[1] // keys.shape[1]
    scale = HEAD_FEATURES ** (-0.5) * LOG2_E
    dma = pltpu.SemaphoreType.DMA
    anywhere = pl.BlockSpec(memory_space=pl.ANY)
    vmem = pl.BlockSpec(memory_space=pltpu.VMEM)
    return pl.pallas_call(
        functools.partial(gather_attend_kernel, depth, early, scale),
        out_shape=(
            jax.ShapeDtypeStruct(queries.shape, queries.dtype),
            jax.ShapeDtypeStruct((depth, early, weight.shape[1]), weight.dtype),
        ),
        in_specs=[pl.BlockSpec(memory_space=pltpu.SMEM), vmem, vmem, vmem, anywhere],
        out_specs=(vmem, anywhere),
        scratch_shapes=[
            pltpu.VMEM((blocks,) + keys.shape, keys.dtype),
            pltpu.VMEM((blocks,) + values.shape, values.dtype),
            pltpu.VMEM((groups, HEAD_FEATURES, lanes), queries.dtype),
            pltpu.VMEM((groups, 1, lanes), jnp.float32),
            pltpu.VMEM((groups, HEAD_FEATURES + 16, lanes), jnp.float32),
            dma((1,)), dma((2, depth, 2)), dma((2, depth, 2)), dma((2, depth)),
            dma((2, blocks)), dma((depth, 2)), dma((depth,)),
        ],
        compiler_params=pltpu.CompilerParams(
            collective_id=0, has_side_effects=True, vmem_limit_bytes=vmem_limit
        ),
    )(placement, queries, keys, values, weight)


def project_kernel(depth, half, hid_ref, w_ref, w_first, out_ref,
                   hid, w_late, theirs, mine_half, other_half, final, landed,
                   own_sem, hid_send, relay_send, hid_recv, w_send, w_recv,
                   core_send, core_recv, out_send, out_recv):
    z, p, px, py, pd = place_of(depth)
    me = z * PLANE + p
    core = lax.axis_index("head")
    rows = hid_ref.shape[0]
    cols = w_ref.shape[1]
    share = depth // 2
    barrier = pltpu.get_barrier_semaphore()
    greeted = (
        z * PLANE + px, z * PLANE + py, z * PLANE + pd,
        (z + 1) % depth * PLANE + p, (z + depth - 1) % depth * PLANE + p,
    )
    for other in greeted:
        pl.semaphore_signal(barrier, inc=1, device_id={"ctx": other}, device_id_type=MESH)
    pl.semaphore_signal(barrier, inc=1, device_id={"head": 1 - core}, device_id_type=MESH)
    pl.semaphore_wait(barrier, len(greeted) + 1)

    copies = Copies()
    always = z >= 0
    above = z + 1 < depth
    below = z > 0
    own_parts = [hid_ref.at[:, pl.ds(s * half, half)] for s in range(2)]
    early = w_first.shape[1]
    w_own = w_ref.at[pl.ds(early, 2 * half - early), :]

    def send_hidden(part, axis):
        target = z * PLANE + (px if axis == 0 else py)
        return remote(own_parts[part], hid.at[p, part], hid_send.at[part, axis], hid_recv.at[p, part], target)

    def relay_hidden(part):
        source, target = (px, py) if part == 0 else (py, px)
        slot = hid.at[source, part]
        return remote(slot, slot, relay_send.at[part], hid_recv.at[source, part], z * PLANE + target)

    def hidden_arrived(source, part):
        slot = hid.at[source, part]
        remote(slot, slot, own_sem.at[0], hid_recv.at[source, part], me).wait_recv()

    def weight(zs, own, up):
        target = (z + 1 if up else z - 1) * PLANE + p
        dst = w_late.at[zs]
        return remote(w_own if own else dst, dst, w_send.at[zs, int(up)], w_recv.at[zs], target)

    for part in range(2):
        copies.start(always, functools.partial(send_hidden, part, part))
    copies.start(above, functools.partial(weight, z, True, True))
    copies.start(below, functools.partial(weight, z, True, False))
    for part in range(2):
        copies.start(always, functools.partial(send_hidden, part, 1 - part))
    locals_ = [pltpu.make_async_copy(own_parts[s], hid.at[p, s], own_sem.at[s]) for s in range(2)]
    locals_.append(pltpu.make_async_copy(w_own, w_late.at[z], own_sem.at[2]))
    for copy in locals_:
        copy.start()

    def pass_weight(t):
        for up in (True, False):
            zs = z - t if up else z + t
            there = z >= t if up else zs < depth

            @pl.when(there)
            def _(zs=zs):
                remote(w_late.at[zs], w_late.at[zs], own_sem.at[0], w_recv.at[zs], me).wait_recv()

            copies.start(there & (above if up else below), functools.partial(weight, zs, False, up))

    for t in range(1, depth):
        pass_weight(t)
        if t == 1:
            for part in range(2):
                hidden_arrived(px if part == 0 else py, part)
                copies.start(always, functools.partial(relay_hidden, part))
    for copy in locals_:
        copy.wait()

    def term(source, chunk):
        return (
            jnp.dot(hid[source, 0], w_first[chunk, :half], preferred_element_type=jnp.float32)
            + jnp.dot(
                hid[source, 1, :, :early - half], w_first[chunk, half:],
                preferred_element_type=jnp.float32,
            )
            + jnp.dot(
                hid[source, 1, :, early - half:], w_late[chunk],
                preferred_element_type=jnp.float32,
            )
        ).astype(jnp.bfloat16)

    def core_copy(slot):
        return pltpu.make_async_remote_copy(
            src_ref=other_half.at[slot], dst_ref=theirs.at[slot],
            send_sem=core_send.at[slot], recv_sem=core_recv.at[slot],
            device_id={"head": 1 - core}, device_id_type=MESH,
        )

    def finished(slot, target):
        return remote(final.at[slot], landed.at[p], out_send.at[slot], out_recv.at[p], z * PLANE + target)

    order = (p, px, py, pd)

    def settle(slot):
        core_copy(slot).wait_recv()
        summed = (
            mine_half[slot].astype(jnp.float32) + theirs[slot].astype(jnp.float32)
        ).astype(jnp.bfloat16)
        if slot == 0:
            landed[p] = summed
        else:
            final[slot] = summed
            copies.start(always, functools.partial(finished, slot, order[slot]))

    for slot, source in enumerate(order):
        if slot in (1, 2):
            hidden_arrived(source, 2 - slot)
        if slot == 3:
            hidden_arrived(source, 0)
            hidden_arrived(source, 1)
        for j in range(share):
            other_half[slot, j] = term(source, (1 - core) * share + j)
        core_copy(slot).start()
        for j in range(share):
            mine_half[slot, j] = term(source, core * share + j)
        if slot:
            settle(slot - 1)
    settle(PLANE - 1)
    for slot in range(1, PLANE):
        source = order[slot]
        remote(landed.at[source], landed.at[source], own_sem.at[0], out_recv.at[source], me).wait_recv()
    for source in range(PLANE):
        for j in range(share):
            at = (j * PLANE + source) * cols
            out_ref[:, at:at + cols] = landed[source, j]
    for slot in range(PLANE):
        core_copy(slot).wait_send()
    copies.finish()


def project(depth, half, hidden, weight, w_first):
    rows, width = hidden.shape
    cols = weight.shape[1]
    share = depth // 2
    dma = pltpu.SemaphoreType.DMA
    vmem = pl.BlockSpec(memory_space=pltpu.VMEM)
    block = pltpu.VMEM((PLANE, share, rows, cols), jnp.bfloat16)
    return pl.pallas_call(
        functools.partial(project_kernel, depth, half),
        out_shape=jax.ShapeDtypeStruct((rows, share * PLANE * cols), hidden.dtype),
        in_specs=[vmem] * 3,
        out_specs=vmem,
        scratch_shapes=[
            pltpu.VMEM((PLANE, 2, rows, half), jnp.bfloat16),
            pltpu.VMEM((depth, 2 * half - w_first.shape[1], cols), jnp.bfloat16),
            block, block, block, block, block,
            dma((3,)), dma((2, 2)), dma((2,)), dma((PLANE, 2)), dma((depth, 2)), dma((depth,)),
            dma((PLANE,)), dma((PLANE,)), dma((PLANE,)), dma((PLANE,)),
        ],
        compiler_params=pltpu.CompilerParams(
            collective_id=1, has_side_effects=True, vmem_limit_bytes=vmem_limit
        ),
    )(hidden, weight, w_first)


def body(fast, placement, queries, keys, values, weight):
    blocks = placement.shape[0]
    depth = blocks // PLANE
    half = weight.shape[0] // 2
    early = half + half // 4
    table = jnp.arange(blocks, dtype=jnp.int32)
    own_block = jnp.sum(jnp.where(table == lax.axis_index("ctx"), placement, 0))[None]
    if fast:
        hidden, w_first = gather_attend(depth, early, placement, queries, keys, values, weight)
        return project(depth, half, hidden, weight, w_first)
    all_keys = lax.all_gather(keys, "ctx", axis=0)
    all_values = lax.all_gather(values, "ctx", axis=0)
    hidden = attend(placement, own_block, queries, all_keys, all_values)
    partial_sum = jnp.dot(
        hidden,
        lax.all_gather(weight, "ctx", axis=1, tiled=True),
        preferred_element_type=jnp.float32,
    )
    term = lax.optimization_barrier(partial_sum.astype(jnp.bfloat16))
    return lax.psum_scatter(term, "head", scatter_dimension=1, tiled=True)


def solution(mesh):
    placed = (P(), P("ctx", "head"), P("ctx", "head"), P("ctx", "head"), P("head", "ctx"))
    fast = mesh.shape["head"] == 2 and mesh.shape["ctx"] == 4 * PLANE
    return jax.shard_map(
        functools.partial(body, fast), mesh=mesh, in_specs=placed,
        out_specs=P("ctx", "head"), check_vma=False,
    )
```
